32 devices in a mesh: tm: 2 (over y), freq: 4 (over z), dish: 4 (over x, core).
Axes of the slice: x: 2, y: 2, z: 4, core: 2. Of those that a mesh axis runs over, the one named last changes fastest.
Arguments:
- time_data: bfloat16 [64, 512, 1024], P('dish', 'freq', 'tm'), may hold values from -24 to 24
- pointing: bfloat16 [8, 128, 128], P('tm'), may hold values from -0.5 to 0.5
- coverage: int32 [8], P('tm'), may hold values from 0 to 15
- noise_inv: bfloat16 [64, 128, 128], P('dish'), as said below
- gains: float32 [64, 512, 8], P('dish', 'freq', 'tm'), may hold values from 0.1 to 1.9
- prior_inv: float32 [512, 512], replicated, as said below
- precond: float32 [512, 2048], P('freq', ('tm', 'dish')), may hold values from 0.5 to 200
Outputs:
- map_estimate: float32 [512, 2048], P('freq', ('tm', 'dish'))
- residual: float32 [512, 2048], P('freq', ('tm', 'dish'))
The draws below stay inside these ranges and needn't reach their ends.
Inputs may be any that keep to these rules, and one draw needn't show every extreme that they name: `noise_inv`: each matrix is symmetric with a positive diagonal that dominates its row, and zero where two samples lie more than 16 apart. `prior_inv`: symmetric with a positive diagonal that dominates its row.
All inputs are finite; a program needn't handle non-finite values.
Results may differ from the reference program's by a relative error of at most 0.0045.
Values may be sent and summed in bfloat16 or wider, within the bound.
A program may use at most 64 MiB of HBM per device.

```python
import math
import jax
import jax.numpy as jnp
from jax import lax

CHANNELS = 512
BLK_DEV = 4
BAND = 16
ITERS = 4
DISHES = 64
BLOCKS = 8
SAMPLES = 1024
REG = 8
TILES = 16
NPIX = 2048


def draw_coverage(key, part):
    subkeys = jax.random.split(key, 5)
    spans = BLOCKS // BLK_DEV
    block_index = jnp.arange(BLOCKS, dtype=jnp.int32)
    span_index = block_index // BLK_DEV
    position = block_index % BLK_DEV
    spread_values = jax.random.randint(subkeys[0], (BLOCKS,), 0, 2 * REG)
    hot_values = jax.random.randint(subkeys[1], (spans,), 0, 2 * REG)
    picked = jax.random.randint(subkeys[2], (BLOCKS,), 0, 2)
    own_values = jax.random.randint(subkeys[3], (BLOCKS,), 0, REG)
    next_values = jax.random.randint(subkeys[4], (BLOCKS,), REG, 2 * REG)
    values = jnp.where(picked == 1, hot_values[span_index], spread_values)
    values = jnp.where(position == 0, own_values, values)
    values = jnp.where(position == 1, next_values, values)
    values = jnp.where(block_index == 0, 0, values)
    values = jnp.where(block_index == 1, 2 * REG - 1, values)
    return values.astype(jnp.int32)


def draw_noise_inv(key, part):
    subkeys = jax.random.split(key, 3)
    raw_values = jax.random.uniform(subkeys[0], (DISHES, 128, 128), jnp.float32, -1.0, 1.0)
    symmetric = 0.5 * (raw_values + jnp.swapaxes(raw_values, 1, 2))
    samples = jnp.arange(128, dtype=jnp.int32)
    distance = jnp.abs(samples[:, None] - samples[None, :])
    inside = (distance <= BAND) & (distance > 0)
    noise_level = jax.random.uniform(subkeys[1], (DISHES, 1, 1), jnp.float32, 0.5, 2.0)
    diagonal = 1.0 + 0.5 * jax.random.uniform(subkeys[2], (DISHES, 128, 1), jnp.float32)
    matrix = jnp.where(inside, symmetric / (2.5 * BAND), 0.0) + jnp.where(distance == 0, diagonal, 0.0)
    return (noise_level / DISHES * matrix).astype(jnp.bfloat16)


def draw_prior_inv(key, part):
    subkeys = jax.random.split(key, 2)
    raw_values = jax.random.uniform(subkeys[0], (CHANNELS, CHANNELS), jnp.float32, -1.0, 1.0)
    symmetric = 0.5 * (raw_values + raw_values.T)
    channel_ids = jnp.arange(CHANNELS, dtype=jnp.int32)
    apart = channel_ids[:, None] != channel_ids[None, :]
    diagonal = 3.5 + 2.0 * jax.random.uniform(subkeys[1], (CHANNELS, 1), jnp.float32)
    return jnp.where(apart, symmetric * (3.0 / CHANNELS), 0.0) + jnp.where(apart, 0.0, diagonal)


def draw_precond(key, part):
    col_level = jnp.arange(NPIX, dtype=jnp.float32)[None, :] / NPIX
    row_level = jnp.arange(CHANNELS, dtype=jnp.float32)[:, None] / CHANNELS
    base_values = jnp.exp(jax.random.uniform(key, (CHANNELS, NPIX), jnp.float32, math.log(0.5), math.log(2.0)))
    return base_values * jnp.power(10.0, col_level) * jnp.power(10.0, row_level)


def steps_of(stream_key, extent, cuts, low, high):
    loudness, own = 1.0, jax.random.fold_in(stream_key, 6)
    for dim, parts in cuts:
        steps = jnp.exp(jax.random.uniform(jax.random.fold_in(own, dim), (parts,), jnp.float32, low / len(cuts), high / len(cuts)))
        loudness = loudness * jnp.repeat(steps, extent[dim] // parts).reshape([-1 if axis == dim else 1 for axis in range(len(extent))])
    return loudness


def centred(stream_key, dims, width, limit, cuts=(), kind=jnp.bfloat16):
    factor_of = steps_of(stream_key, dims, cuts, -0.22, 0.18) if cuts else 1.0
    array = jax.random.normal(stream_key, dims, jnp.float32) * width * factor_of
    return jnp.minimum(jnp.maximum(array, -limit), limit).astype(kind)


def setup_inputs(seed: int = 0) -> dict:
    key_of = jax.random.split(jax.random.key(seed), 8)
    time_data = centred(key_of[0], (DISHES, CHANNELS, SAMPLES), 4.0, 24.0, ((0, 4), (1, 4), (2, 2)))
    pointing = centred(key_of[1], (BLOCKS, 128, 128), 128 ** -0.5, 0.5, ((0, 2),))
    coverage = draw_coverage(jax.random.fold_in(key_of[7], 71), 0)
    noise_inv = draw_noise_inv(jax.random.fold_in(key_of[7], 71), 0)
    gains = jnp.clip(1.0 + 0.18 * jax.random.normal(key_of[4], (DISHES, CHANNELS, BLOCKS), jnp.float32), 0.1, 1.9)
    prior_inv = draw_prior_inv(jax.random.fold_in(key_of[7], 71), 0)
    precond = draw_precond(jax.random.fold_in(key_of[7], 71), 0)
    return {"time_data": time_data, "pointing": pointing, "coverage": coverage, "noise_inv": noise_inv, "gains": gains, "prior_inv": prior_inv, "precond": precond}


def reference(time_data, pointing, coverage, noise_inv, gains, prior_inv, precond):
    highest = lax.Precision.HIGHEST
    scan_index = jnp.arange(BLOCKS, dtype=jnp.int32) // BLK_DEV
    tile_of = ((scan_index * REG + coverage) % TILES).astype(jnp.int32)
    point_wide = pointing.astype(jnp.float32)

    def back_project(weighted):
        rounded = lax.optimization_barrier(weighted.astype(jnp.bfloat16)).astype(jnp.float32)
        tile_part = jnp.einsum("cbt,bti->cbi", rounded, point_wide, precision=highest)
        summed = jnp.zeros((CHANNELS, TILES, 128), jnp.float32).at[:, tile_of, :].add(tile_part)
        return summed.reshape(CHANNELS, NPIX)

    def data_term(map_field):
        rounded = lax.optimization_barrier(map_field.astype(jnp.bfloat16)).astype(jnp.float32)
        tile_maps = rounded.reshape(CHANNELS, TILES, 128)[:, tile_of, :]
        model_tod = jnp.einsum("cbp,bsp->cbs", tile_maps, point_wide, precision=highest)
        model_tod = lax.optimization_barrier(model_tod.astype(jnp.bfloat16)).astype(jnp.float32)

        def dish_step(running, dish_items):
            weight, matrix = dish_items
            dish_term = jnp.einsum("cbs,st->cbt", model_tod, matrix.astype(jnp.float32), precision=highest)
            return running + (weight * weight)[:, :, None] * dish_term, None

        mixed_tod, unused = lax.scan(dish_step, jnp.zeros((CHANNELS, BLOCKS, 128), jnp.float32), (gains, noise_inv))
        return back_project(mixed_tod)

    def operate(map_field):
        return data_term(map_field) + jnp.dot(prior_inv, map_field, precision=highest)

    def rhs_step(running, dish_items):
        weight, matrix, series = dish_items
        blocked = series.astype(jnp.float32).reshape(CHANNELS, BLOCKS, 128)
        dish_term = jnp.einsum("cbs,st->cbt", blocked, matrix.astype(jnp.float32), precision=highest)
        return running + weight[:, :, None] * dish_term, None

    rhs_tod, unused = lax.scan(rhs_step, jnp.zeros((CHANNELS, BLOCKS, 128), jnp.float32), (gains, noise_inv, time_data))
    right_side = back_project(rhs_tod)
    estimate = jnp.zeros_like(right_side)
    residual = right_side
    scaled = precond * residual
    direction = scaled
    energy_now = jnp.sum(residual * scaled)
    for iteration in range(ITERS):
        operated = operate(direction)
        step_size = energy_now / jnp.sum(direction * operated)
        estimate = estimate + step_size * direction
        residual = residual - step_size * operated
        if iteration + 1 < ITERS:
            scaled = precond * residual
            energy_next = jnp.sum(residual * scaled)
            direction = scaled + (energy_next / energy_now) * direction
            energy_now = energy_next
    return estimate, residual
```

```python
import functools

import jax
import jax.numpy as jnp
from jax import lax
from jax.experimental import pallas as pl
from jax.experimental.pallas import tpu as pltpu
from jax.sharding import PartitionSpec as P

ITERS = 4
BAND = 16
DIAGS = 2 * BAND + 1
ROWS = 16
LANES = 128
MESH = pl.DeviceIdType.MESH


def shifted(block, axis, distance):
    devices = range(lax.axis_size(axis))
    route = [((i - distance) % len(devices), i) for i in devices]
    return lax.ppermute(block, axis, route)


def general_body(time_data, pointing, coverage, noise_inv, gains, prior_inv, precond):
    highest = lax.Precision.HIGHEST
    channels_dev = precond.shape[0]
    owned_pixels = precond.shape[1]
    blocks_dev = pointing.shape[0]
    dish_count = lax.axis_size("dish")
    owned_tiles = owned_pixels // 128
    region_tiles = owned_tiles * dish_count
    window_tiles = 2 * region_tiles
    tile_count = jnp.arange(owned_tiles, dtype=jnp.int32)
    first_owned = lax.axis_index("dish") * owned_tiles + tile_count
    wanted = jnp.concatenate([first_owned, first_owned + region_tiles])
    own_hot = (coverage[:, None] == wanted[None, :]).astype(jnp.float32)

    def collect(partial_tod):
        summed = lax.psum(partial_tod, "dish")
        tile_part = jnp.einsum(
            "cbt,bti->cbi",
            summed.astype(jnp.bfloat16),
            pointing,
            preferred_element_type=jnp.float32,
        )
        window = jnp.einsum("cbi,bw->cwi", tile_part, own_hot, precision=highest)
        own_part = window[:, :owned_tiles, :].reshape(channels_dev, owned_pixels)
        ahead_part = window[:, owned_tiles:, :].reshape(channels_dev, owned_pixels)
        arrived = shifted(ahead_part, "tm", 1)
        return own_part + arrived

    def energy_of(residual, scaled):
        return lax.psum(jnp.sum(residual * scaled), ("tm", "freq", "dish"))

    series = time_data.reshape(time_data.shape[0], channels_dev, blocks_dev, 128)
    rhs_weighted = jnp.einsum(
        "dcbs,dst->dcbt", series, noise_inv, preferred_element_type=jnp.float32
    )
    right_side = collect(jnp.sum(gains[:, :, :, None] * rhs_weighted, axis=0))
    estimate = jnp.zeros_like(right_side)
    residual = right_side
    scaled = precond * residual
    direction = scaled
    energy_now = energy_of(residual, scaled)
    for iteration in range(ITERS):
        swapped = lax.all_to_all(direction, "freq", split_axis=1, concat_axis=0, tiled=True)
        applied = jnp.dot(prior_inv, swapped, precision=highest, preferred_element_type=jnp.float32)
        region_map = lax.all_gather(direction.astype(jnp.bfloat16), "dish", axis=1, tiled=True)
        following = shifted(region_map, "tm", -1)
        data_window = jnp.concatenate([region_map, following], axis=1)
        tile_maps = data_window.reshape(channels_dev, window_tiles, 128)[:, coverage, :]
        model_tod = jnp.einsum(
            "cbp,bsp->cbs", tile_maps, pointing, preferred_element_type=jnp.float32
        ).astype(jnp.bfloat16)
        weighted = jnp.einsum(
            "cbs,dst->dcbt", model_tod, noise_inv, preferred_element_type=jnp.float32
        )
        mixed_part = jnp.sum((gains * gains)[:, :, :, None] * weighted, axis=0)
        operated = collect(mixed_part) + lax.all_to_all(
            applied, "freq", split_axis=0, concat_axis=1, tiled=True
        )
        curve_sum = lax.psum(jnp.sum(direction * operated), ("tm", "freq", "dish"))
        step_size = energy_now / curve_sum
        estimate = estimate + step_size * direction
        residual = residual - step_size * operated
        if iteration + 1 < ITERS:
            scaled = precond * residual
            energy_next = energy_of(residual, scaled)
            direction = scaled + energy_next / energy_now * direction
            energy_now = energy_next
    return (estimate, residual)


def halves(value):
    high = value.astype(jnp.bfloat16).astype(jnp.float32)
    return high, value - high


def scalar_rows(part):
    high, rest = halves(part)
    middle, low = halves(rest)
    row = lax.broadcasted_iota(jnp.int32, (8, LANES), 0)
    return jnp.where(
        row == 0, high, jnp.where(row == 1, middle, jnp.where(row == 2, low, 0.0))
    )


def total(value):
    return jnp.sum(jnp.sum(value, axis=0, keepdims=True), axis=1, keepdims=True)


def kernel(
    sizes, msg, diag_in, pointing, tile_in, prior, prior_diag, x_out, r_out,
    got, diags, points, tiles_at, mixing, model, state_x, state_r, state_u,
    state_p, state_s, state_w, pre, out_send, out_recv, back_send, back_recv,
    end_send, end_recv, setup_sems, leg_sems,
):
    tm, freq, dish, blocks_dev, tiles, tiles_own = sizes
    group = tm * dish
    devices = group * freq
    blocks = tm * blocks_dev
    span_rows = blocks_dev * ROWS
    my_tm = lax.axis_index("tm")
    my_freq = lax.axis_index("freq")
    my_dish = lax.axis_index("dish")
    member = my_tm * dish + my_dish
    me = my_freq * group + member

    def place(q):
        rest = lax.rem(q, group)
        return {
            "tm": lax.div(rest, dish),
            "freq": lax.div(q, group),
            "dish": lax.rem(rest, dish),
        }

    def remote(src, dst, send, recv, where):
        return pltpu.make_async_remote_copy(
            src_ref=src, dst_ref=dst, send_sem=send, recv_sem=recv,
            device_id=where, device_id_type=MESH,
        )

    def wait_bytes(ref, sem):
        pltpu.make_async_copy(ref, ref, sem).wait()

    barrier = pltpu.get_barrier_semaphore()

    def greet(step, carry):
        q = lax.rem(me + step, devices)
        pl.semaphore_signal(barrier, inc=1, device_id=place(q), device_id_type=MESH)
        return carry

    lax.fori_loop(1, devices, greet, 0)
    pl.semaphore_wait(barrier, devices - 1)

    for step in range(1, group):
        t = lax.rem(member + step, group)
        remote(
            msg.at[t], got.at[member], setup_sems.at[0], setup_sems.at[1],
            place(my_freq * group + t),
        ).start()
    for step in range(1, dish):
        t = lax.rem(my_dish + step, dish)
        remote(
            diag_in, diags.at[my_dish], setup_sems.at[2], setup_sems.at[3],
            {"tm": my_tm, "freq": my_freq, "dish": t},
        ).start()
    for step in range(1, tm):
        t = lax.rem(my_tm + step, tm)
        where = {"tm": t, "freq": my_freq, "dish": my_dish}
        remote(pointing, points.at[my_tm], setup_sems.at[4], setup_sems.at[5], where).start()
        remote(tile_in, tiles_at.at[my_tm], setup_sems.at[6], setup_sems.at[7], where).start()
    got[member] = msg[member]
    diags[my_dish] = diag_in[...]
    points[my_tm] = pointing[...]
    tiles_at[my_tm] = tile_in[...]

    wait_bytes(got.at[pl.ds(0, group - 1)], setup_sems.at[1])
    wait_bytes(diags.at[pl.ds(0, dish - 1)], setup_sems.at[3])
    if tm > 1:
        wait_bytes(points.at[pl.ds(0, tm - 1)], setup_sems.at[5])
        wait_bytes(tiles_at.at[pl.ds(0, tm - 1)], setup_sems.at[7])

    gain_first = span_rows
    gain_list = []
    for j in range(dish):
        column = got[j, gain_first:gain_first + ROWS]
        for k in range(1, tm):
            column = column + got[k * dish + j, gain_first:gain_first + ROWS]
        gain_list.append(column)
    gain = jnp.concatenate(gain_list, axis=0)
    high, low = halves(gain * gain)
    weights = jnp.concatenate([high, low], axis=0).T.astype(jnp.bfloat16)

    def mix(k, carry):
        one = [diags[j, k] for j in range(dish)]
        stacked = jnp.concatenate(one + one, axis=0)
        mixing[k] = jnp.dot(weights, stacked, preferred_element_type=jnp.float32)
        return carry

    lax.fori_loop(0, DIAGS, mix, 0)

    def tile_row(b):
        row = tiles_at[b // blocks_dev, pl.ds(b % blocks_dev, 1), :]
        return jnp.broadcast_to(row, (ROWS, LANES))

    def back_project(rows):
        parts = [
            jnp.dot(
                rows[b * ROWS:(b + 1) * ROWS], points[b // blocks_dev, b % blocks_dev],
                preferred_element_type=jnp.float32,
            )
            for b in range(blocks)
        ]
        rows_at = [tile_row(b) for b in range(blocks)]
        summed = []
        for t in range(tiles):
            one = jnp.where(rows_at[0] == t, parts[0], 0.0)
            for b in range(1, blocks):
                one = one + jnp.where(rows_at[b] == t, parts[b], 0.0)
            summed.append(one)
        return summed

    rhs_list = []
    for k in range(tm):
        span = got[k * dish, 0:span_rows]
        for j in range(1, dish):
            span = span + got[k * dish + j, 0:span_rows]
        rhs_list.append(span)
    rhs = jnp.concatenate(rhs_list, axis=0).astype(jnp.bfloat16)
    pre_first = span_rows + ROWS
    for t, one in enumerate(back_project(rhs)):
        first = pre_first + (t % tiles_own) * ROWS
        scale = got[t // tiles_own, first:first + ROWS]
        pre[t] = scale
        state_r[t] = one
        state_u[t] = scale * one
    zero = jnp.zeros((tiles, ROWS, LANES), jnp.float32)
    state_x[...] = zero
    state_p[...] = zero
    state_s[...] = zero

    half = LANES // 2

    def left_of(shape):
        return lax.broadcasted_iota(jnp.int32, shape, len(shape) - 1) < half

    def send_all(src, dst, send, recv):
        def step_of(step, carry):
            q = lax.rem(me + step, devices)
            remote(src.at[q], dst.at[me], send, recv, place(q)).start()
            return carry

        lax.fori_loop(1, devices, step_of, 0)

    def iteration(index, carry):
        gamma_old, alpha_old = carry
        left = left_of((8, LANES))
        first = state_r[...] * state_u[...]
        gamma_rows = scalar_rows(jnp.sum(jnp.sum(first, axis=0), axis=0, keepdims=True))
        for t in range(tiles):
            upper, lower = state_u[t, 0:8], state_u[t, 8:16]
            front = jnp.where(left, upper, pltpu.roll(lower, half, 1))
            back = jnp.where(left, pltpu.roll(upper, half, 1), lower)
            out_send[2 * t] = jnp.concatenate([front, gamma_rows], axis=0).astype(jnp.bfloat16)
            out_send[2 * t + 1] = jnp.concatenate([back, gamma_rows], axis=0).astype(jnp.bfloat16)
        send_all(out_send, out_recv, leg_sems.at[0], leg_sems.at[1])
        out_recv[me] = out_send[me]

        for b in range(blocks):
            row = tile_row(b)
            seen = jnp.where(row == 0, state_u[0], 0.0)
            for t in range(1, tiles):
                seen = seen + jnp.where(row == t, state_u[t], 0.0)
            model[b * ROWS:(b + 1) * ROWS] = lax.dot_general(
                seen.astype(jnp.bfloat16), points[b // blocks_dev, b % blocks_dev],
                (((1,), (1,)), ((), ())), preferred_element_type=jnp.float32,
            ).astype(jnp.bfloat16).astype(jnp.float32)
        tod = model[...]
        mixed = mixing[BAND] * tod
        for k in range(DIAGS):
            if k != BAND:
                mixed = mixed + mixing[k] * pltpu.roll(tod, (BAND - k) % LANES, 1)
        diagonal = prior_diag[...]
        dots = jnp.zeros((ROWS, LANES), jnp.float32)
        for t, one in enumerate(back_project(mixed.astype(jnp.bfloat16))):
            here = state_u[t]
            term = one + diagonal * here
            state_w[t] = term
            dots = dots + here * term

        wait_bytes(out_recv.at[pl.ds(0, devices - 1)], leg_sems.at[1])
        field = out_recv[...]
        wide = field.astype(jnp.float32)
        gamma = total(jnp.sum(wide[:, 8:16], axis=0))
        product = jnp.dot(
            prior[...], field.reshape(devices * ROWS, LANES),
            preferred_element_type=jnp.float32,
        ).reshape(2, devices, 2, 8, LANES)
        left = left_of((devices, 8, LANES))
        applied = jnp.where(left, product[0, :, 0], product[1, :, 1]) + pltpu.roll(
            jnp.where(left, product[0, :, 1], product[1, :, 0]), half, 2
        )
        dots = jnp.sum(dots, axis=0, keepdims=True) + jnp.sum(
            jnp.sum(applied * wide[:, 0:8], axis=0), axis=0, keepdims=True
        )
        delta_rows = jnp.broadcast_to(scalar_rows(dots)[None], (devices, 8, LANES))
        back_send[...] = jnp.concatenate([applied, delta_rows], axis=1).astype(jnp.bfloat16)
        send_all(back_send, back_recv, leg_sems.at[2], leg_sems.at[3])
        back_recv[me] = back_send[me]
        beta = jnp.where(index == 0, 0.0, gamma / gamma_old)
        state_p[...] = state_u[...] + beta[None] * state_p[...]

        wait_bytes(back_recv.at[pl.ds(0, devices - 1)], leg_sems.at[3])
        wide = back_recv[...].astype(jnp.float32)
        delta = total(jnp.sum(wide[:, 8:16], axis=0))
        alpha = gamma / (delta - beta * gamma / alpha_old)
        left = left_of((8, LANES))
        for t in range(tiles):
            front, back = wide[2 * t, 0:8], wide[2 * t + 1, 0:8]
            upper = jnp.where(left, front, pltpu.roll(back, half, 1))
            lower = jnp.where(left, pltpu.roll(front, half, 1), back)
            operated = state_w[t] + jnp.concatenate([upper, lower], axis=0) + beta * state_s[t]
            state_s[t] = operated
            state_x[t] = state_x[t] + alpha * state_p[t]
            residual = state_r[t] - alpha * operated
            state_r[t] = residual
            state_u[t] = pre[t] * residual
        wait_bytes(out_send.at[pl.ds(0, devices - 1)], leg_sems.at[0])
        wait_bytes(back_send.at[pl.ds(0, devices - 1)], leg_sems.at[2])
        return gamma, alpha

    one = jnp.ones((1, 1), jnp.float32)
    lax.fori_loop(0, ITERS, iteration, (one, one))

    for t in range(tiles):
        first = (t % tiles_own) * LANES
        end_send[t // tiles_own, 0, :, first:first + LANES] = state_x[t]
        end_send[t // tiles_own, 1, :, first:first + LANES] = state_r[t]
    for step in range(1, group):
        t = lax.rem(member + step, group)
        remote(
            end_send.at[t], end_recv.at[member], setup_sems.at[8], setup_sems.at[9],
            place(my_freq * group + t),
        ).start()
    end_recv[member] = end_send[member]
    wait_bytes(msg.at[pl.ds(0, group - 1)], setup_sems.at[0])
    for step in range(1, dish):
        wait_bytes(diag_in, setup_sems.at[2])
    for step in range(1, tm):
        wait_bytes(pointing, setup_sems.at[4])
        wait_bytes(tile_in, setup_sems.at[6])
    wait_bytes(end_recv.at[pl.ds(0, group - 1)], setup_sems.at[9])
    for t in range(group):
        x_out[t * ROWS:(t + 1) * ROWS] = end_recv[t, 0]
        r_out[t * ROWS:(t + 1) * ROWS] = end_recv[t, 1]
    wait_bytes(end_send.at[pl.ds(0, group - 1)], setup_sems.at[8])


def local_body(time_data, pointing, coverage, noise_inv, gains, prior_inv, precond):
    tm, freq, dish = (lax.axis_size(name) for name in ("tm", "freq", "dish"))
    group = tm * dish
    devices = group * freq
    dishes_dev, channels_dev, _ = time_data.shape
    channels = prior_inv.shape[0]
    blocks_dev = pointing.shape[0]
    tiles_own = precond.shape[1] // LANES
    tiles = tiles_own * group
    span_rows = blocks_dev * ROWS
    my_tm = lax.axis_index("tm")
    me = lax.axis_index("freq") * group + my_tm * dish + lax.axis_index("dish")

    series = time_data.reshape(dishes_dev, channels_dev, blocks_dev, LANES)
    weighted = jnp.einsum(
        "dcbs,dst->dcbt", series, noise_inv, preferred_element_type=jnp.float32
    )
    rhs = jnp.sum(gains[:, :, :, None] * weighted, axis=0)
    rhs = rhs.reshape(group, ROWS, blocks_dev, LANES).transpose(0, 2, 1, 3)
    gain = gains.reshape(dishes_dev, group, ROWS, blocks_dev).transpose(1, 0, 3, 2)
    gain = jnp.tile(gain.reshape(group, dishes_dev, span_rows), (1, 1, tm))
    lane = jnp.arange(LANES, dtype=jnp.int32)
    gain = jnp.where(lane // span_rows == my_tm, gain, 0.0)
    scale = precond.reshape(group, ROWS, tiles_own, LANES).transpose(0, 2, 1, 3)
    msg = jnp.concatenate(
        [
            rhs.reshape(group, span_rows, LANES),
            gain,
            scale.reshape(group, tiles_own * ROWS, LANES),
        ],
        axis=1,
    )
    apart = lane[:, None] - lane[None, :]
    offsets = jnp.arange(-BAND, BAND + 1, dtype=jnp.int32)
    diag_in = jnp.sum(
        jnp.where(
            (apart[None] == offsets[:, None, None])[:, None], noise_inv[None], 0
        ).astype(jnp.float32),
        axis=2,
    ).astype(jnp.bfloat16)
    tile_of = lax.rem(my_tm * (tiles // tm) + coverage, tiles).astype(jnp.int32)
    tile_in = jnp.broadcast_to(jnp.pad(tile_of, (0, 8 - blocks_dev))[:, None], (8, LANES))
    ids = jnp.arange(channels, dtype=jnp.int32)
    same = ids[:, None] == ids[None, :]
    off = jnp.where(same, 0.0, prior_inv).astype(jnp.bfloat16)
    off = off.reshape(channels, devices, 2, 8)
    off = jnp.pad(off, ((0, 0), (0, 0), (0, 0), (0, 8)))
    prior = jnp.concatenate(
        [off[:, :, h].reshape(channels, devices * ROWS) for h in range(2)], axis=0
    )
    prior_diag = jnp.sum(jnp.where(same, prior_inv, 0.0), axis=1)
    prior_diag = lax.dynamic_slice(prior_diag, (me * ROWS,), (ROWS,))
    prior_diag = jnp.broadcast_to(prior_diag[:, None], (ROWS, LANES))

    f32, bf16 = jnp.float32, jnp.bfloat16
    state = pltpu.VMEM((tiles, ROWS, LANES), f32)
    leg = pltpu.VMEM((devices, ROWS, LANES), bf16)
    end = pltpu.VMEM((group, 2, ROWS, tiles_own * LANES), f32)
    vmem = pl.BlockSpec(memory_space=pltpu.VMEM)
    sizes = (tm, freq, dish, blocks_dev, tiles, tiles_own)
    shape = jax.ShapeDtypeStruct(precond.shape, f32)
    return pl.pallas_call(
        functools.partial(kernel, sizes),
        out_shape=(shape, shape),
        in_specs=[vmem] * 6,
        out_specs=(vmem, vmem),
        scratch_shapes=[
            pltpu.VMEM(msg.shape, f32),
            pltpu.VMEM((dish,) + diag_in.shape, bf16),
            pltpu.VMEM((tm,) + pointing.shape, bf16),
            pltpu.VMEM((tm, 8, LANES), jnp.int32),
            pltpu.VMEM((DIAGS, LANES, LANES), f32),
            pltpu.VMEM((LANES, LANES), f32),
            state, state, state, state, state, state, state,
            leg, leg, leg, leg, end, end,
            pltpu.SemaphoreType.DMA((10,)),
            pltpu.SemaphoreType.DMA((4,)),
        ],
        compiler_params=pltpu.CompilerParams(
            collective_id=0, has_side_effects=True, vmem_limit_bytes=40 * 1024 * 1024
        ),
    )(msg, diag_in, pointing, tile_in, prior, prior_diag)


def body(time_data, pointing, coverage, noise_inv, gains, prior_inv, precond):
    group = lax.axis_size("tm") * lax.axis_size("dish")
    devices = group * lax.axis_size("freq")
    fits = (
        prior_inv.shape[0] == devices * ROWS
        and precond.shape[1] * group * 2 == devices * LANES
        and pointing.shape[0] * lax.axis_size("tm") * ROWS == LANES
        and time_data.shape[0] == ROWS
        and ROWS * lax.axis_size("dish") * 2 == LANES
    )
    run = local_body if fits else general_body
    return run(time_data, pointing, coverage, noise_inv, gains, prior_inv, precond)


def solution(mesh):
    return jax.shard_map(
        body,
        mesh=mesh,
        in_specs=(
            P("dish", "freq", "tm"),
            P("tm", None, None),
            P("tm"),
            P("dish", None, None),
            P("dish", "freq", "tm"),
            P(),
            P("freq", ("tm", "dish")),
        ),
        out_specs=(P("freq", ("tm", "dish")), P("freq", ("tm", "dish"))),
        check_vma=False,
    )
```

```python
import functools

import jax
import jax.numpy as jnp
from jax import lax
from jax.experimental import pallas as pl
from jax.experimental.pallas import tpu as pltpu
from jax.sharding import PartitionSpec as P

ITERS = 4
BAND = 16
DIAGS = 2 * BAND + 1
ROWS = 16
LANES = 128
MESH = pl.DeviceIdType.MESH


def shifted(block, axis, distance):
    devices = range(lax.axis_size(axis))
    route = [((i - distance) % len(devices), i) for i in devices]
    return lax.ppermute(block, axis, route)


def general_body(time_data, pointing, coverage, noise_inv, gains, prior_inv, precond):
    highest = lax.Precision.HIGHEST
    channels_dev = precond.shape[0]
    owned_pixels = precond.shape[1]
    blocks_dev = pointing.shape[0]
    dish_count = lax.axis_size("dish")
    owned_tiles = owned_pixels // 128
    region_tiles = owned_tiles * dish_count
    window_tiles = 2 * region_tiles
    tile_count = jnp.arange(owned_tiles, dtype=jnp.int32)
    first_owned = lax.axis_index("dish") * owned_tiles + tile_count
    wanted = jnp.concatenate([first_owned, first_owned + region_tiles])
    own_hot = (coverage[:, None] == wanted[None, :]).astype(jnp.float32)

    def collect(partial_tod):
        summed = lax.psum(partial_tod, "dish")
        tile_part = jnp.einsum(
            "cbt,bti->cbi",
            summed.astype(jnp.bfloat16),
            pointing,
            preferred_element_type=jnp.float32,
        )
        window = jnp.einsum("cbi,bw->cwi", tile_part, own_hot, precision=highest)
        own_part = window[:, :owned_tiles, :].reshape(channels_dev, owned_pixels)
        ahead_part = window[:, owned_tiles:, :].reshape(channels_dev, owned_pixels)
        arrived = shifted(ahead_part, "tm", 1)
        return own_part + arrived

    def energy_of(residual, scaled):
        return lax.psum(jnp.sum(residual * scaled), ("tm", "freq", "dish"))

    series = time_data.reshape(time_data.shape[0], channels_dev, blocks_dev, 128)
    rhs_weighted = jnp.einsum(
        "dcbs,dst->dcbt", series, noise_inv, preferred_element_type=jnp.float32
    )
    right_side = collect(jnp.sum(gains[:, :, :, None] * rhs_weighted, axis=0))
    estimate = jnp.zeros_like(right_side)
    residual = right_side
    scaled = precond * residual
    direction = scaled
    energy_now = energy_of(residual, scaled)
    for iteration in range(ITERS):
        swapped = lax.all_to_all(direction, "freq", split_axis=1, concat_axis=0, tiled=True)
        applied = jnp.dot(prior_inv, swapped, precision=highest, preferred_element_type=jnp.float32)
        region_map = lax.all_gather(direction.astype(jnp.bfloat16), "dish", axis=1, tiled=True)
        following = shifted(region_map, "tm", -1)
        data_window = jnp.concatenate([region_map, following], axis=1)
        tile_maps = data_window.reshape(channels_dev, window_tiles, 128)[:, coverage, :]
        model_tod = jnp.einsum(
            "cbp,bsp->cbs", tile_maps, pointing, preferred_element_type=jnp.float32
        ).astype(jnp.bfloat16)
        weighted = jnp.einsum(
            "cbs,dst->dcbt", model_tod, noise_inv, preferred_element_type=jnp.float32
        )
        mixed_part = jnp.sum((gains * gains)[:, :, :, None] * weighted, axis=0)
        operated = collect(mixed_part) + lax.all_to_all(
            applied, "freq", split_axis=0, concat_axis=1, tiled=True
        )
        curve_sum = lax.psum(jnp.sum(direction * operated), ("tm", "freq", "dish"))
        step_size = energy_now / curve_sum
        estimate = estimate + step_size * direction
        residual = residual - step_size * operated
        if iteration + 1 < ITERS:
            scaled = precond * residual
            energy_next = energy_of(residual, scaled)
            direction = scaled + energy_next / energy_now * direction
            energy_now = energy_next
    return (estimate, residual)


def halves(value):
    high = value.astype(jnp.bfloat16).astype(jnp.float32)
    return high, value - high


def total(value):
    return jnp.sum(jnp.sum(value, axis=0, keepdims=True), axis=1, keepdims=True)


def kernel(
    sizes, time_data, pointing, coverage, noise, gains, prior, precond, x_out, r_out,
    rhs_sum, rhs_send, rhs_got, gain_send, gain_got, diag_wide, diag_send, diags,
    points, tile_send, tiles_at, pre_got, mixing, model, state_x, state_r, state_u,
    state_p, state_w, pre, tile_p, same_half, other_half, u_send, field, back_send,
    back, fresh_send, fresh_got, curve_send, curve_got, end_send, end_recv, setup_sems, leg_sems,
):
    tm, freq, dish = sizes
    group = tm * dish
    devices = group * freq
    dishes_dev, channels_dev, _ = time_data.shape
    blocks_dev = pointing.shape[0]
    blocks = tm * blocks_dev
    span_rows = blocks_dev * ROWS
    tiles_own = precond.shape[1] // LANES
    tiles = tiles_own * group
    pairs = devices // 2
    my_tm = lax.axis_index("tm")
    my_freq = lax.axis_index("freq")
    my_dish = lax.axis_index("dish")
    member = my_tm * dish + my_dish
    me = my_freq * group + member
    my_pair = lax.div(me, 2)
    my_half = lax.rem(me, 2)

    tm_at = [lax.rem(my_tm + step, tm) for step in range(tm)]
    freq_at = [lax.rem(my_freq + step, freq) for step in range(freq)]
    dish_at = [lax.rem(my_dish + step, dish) for step in range(dish)]
    steps = [
        (a, b, c) for b in range(freq) for a in range(tm) for c in range(dish)
    ]
    steps = sorted(steps[1:], key=lambda s: (-min(s[1], freq - s[1]), s))

    def index_of(step):
        a, b, c = step
        return freq_at[b] * group + tm_at[a] * dish + dish_at[c]

    def place(step):
        a, b, c = step
        return {"tm": tm_at[a], "freq": freq_at[b], "dish": dish_at[c]}

    def remote(src, dst, send, recv, step):
        return pltpu.make_async_remote_copy(
            src_ref=src, dst_ref=dst, send_sem=send, recv_sem=recv,
            device_id=place(step), device_id_type=MESH,
        )

    def wait_bytes(ref, sem):
        pltpu.make_async_copy(ref, ref, sem).wait()

    barrier = pltpu.get_barrier_semaphore()
    for step in steps:
        pl.semaphore_signal(barrier, inc=1, device_id=place(step), device_id_type=MESH)

    at_row = lax.broadcasted_iota(jnp.int32, (LANES, LANES), 0)
    at_column = lax.broadcasted_iota(jnp.int32, (LANES, LANES), 1)
    reverse = jnp.where(at_row + at_column == LANES - 1, 1.0, 0.0).astype(jnp.bfloat16)

    rhs_sum[...] = jnp.zeros_like(rhs_sum)

    def dish_step(d, carry):
        weight = gains[d]
        for b in range(blocks_dev):
            series = time_data[d, :, b * LANES:(b + 1) * LANES]
            term = lax.dot_general(
                noise[d], series, (((1,), (1,)), ((), ())),
                preferred_element_type=jnp.float32,
            )
            rhs_sum[b] += weight[b:b + 1, :] * term
        upside = jnp.dot(reverse, noise[d], preferred_element_type=jnp.float32)
        skewed = pltpu.roll(upside, 1, 1, stride=1, stride_axis=0)
        turned = jnp.dot(
            skewed.T.astype(jnp.bfloat16), reverse, preferred_element_type=jnp.float32
        )
        diag_wide[d, 0:BAND] = turned[LANES - BAND:]
        diag_wide[d, BAND:3 * BAND] = turned[0:2 * BAND]
        return carry

    lax.fori_loop(0, dishes_dev, dish_step, 0)
    for b in range(blocks_dev):
        rhs_send[:, b] = rhs_sum[b].T.reshape(group, ROWS, LANES)
    for k in range(DIAGS):
        diag_send[k] = diag_wide[:, k, :].astype(jnp.bfloat16)
    lane = lax.broadcasted_iota(jnp.int32, (dishes_dev, LANES), 1)
    slot = [
        jnp.logical_and(
            lane >= my_tm * span_rows + b * ROWS, lane < my_tm * span_rows + (b + 1) * ROWS
        )
        for b in range(blocks_dev)
    ]
    for t in range(group):
        column = jnp.zeros((dishes_dev, LANES), jnp.float32)
        for b in range(blocks_dev):
            turn = lax.rem(my_tm * span_rows + (b * ROWS - t * ROWS + LANES), LANES)
            column = jnp.where(slot[b], pltpu.roll(gains[:, b, :], turn, 1), column)
        gain_send[t] = column
    row = lax.broadcasted_iota(jnp.int32, (8, LANES), 0)
    tile_rows = jnp.zeros((8, LANES), jnp.int32)
    for b in range(blocks_dev):
        tile = lax.rem(my_tm * (tiles // tm) + coverage[b], tiles)
        tile_rows = jnp.where(row == b, tile, tile_rows)
    tile_send[...] = tile_rows

    pl.semaphore_wait(barrier, devices - 1)

    group_steps = [step for step in steps if step[1] == 0]
    for step in group_steps:
        t = tm_at[step[0]] * dish + dish_at[step[2]]
        remote(
            rhs_send.at[t], rhs_got.at[member], setup_sems.at[0], setup_sems.at[1], step
        ).start()
        remote(
            precond.at[pl.ds(pl.multiple_of(t * ROWS, ROWS), ROWS), :], pre_got.at[member],
            setup_sems.at[2], setup_sems.at[3], step,
        ).start()
    for a in range(1, tm):
        step = (a, 0, 0)
        remote(tile_send, tiles_at.at[my_tm], setup_sems.at[6], setup_sems.at[7], step).start()
        remote(pointing, points.at[my_tm], setup_sems.at[4], setup_sems.at[5], step).start()
    for step in group_steps:
        t = tm_at[step[0]] * dish + dish_at[step[2]]
        remote(
            gain_send.at[t], gain_got.at[member], setup_sems.at[8], setup_sems.at[9], step
        ).start()
    for c in range(1, dish):
        remote(
            diag_send, diags.at[my_dish], setup_sems.at[10], setup_sems.at[11], (0, 0, c)
        ).start()
    rhs_got[member] = rhs_send[member]
    pre_got[member] = precond[pl.ds(pl.multiple_of(member * ROWS, ROWS), ROWS), :]
    tiles_at[my_tm] = tile_send[...]
    points[my_tm] = pointing[...]
    gain_got[member] = gain_send[member]
    diags[my_dish] = diag_send[...]

    channels = devices * ROWS
    rows_here = pairs * ROWS
    kept = prior[:, my_half].reshape(rows_here, channels)
    at_row = lax.broadcasted_iota(jnp.int32, (rows_here, channels), 0)
    at_column = lax.broadcasted_iota(jnp.int32, (rows_here, channels), 1)
    channel = (at_row // ROWS) * (2 * ROWS) + my_half * ROWS + at_row % ROWS
    kept = jnp.where(channel == at_column, 0.0, kept).astype(jnp.bfloat16)
    at_row = lax.broadcasted_iota(jnp.int32, (channels, rows_here), 0)
    at_column = lax.broadcasted_iota(jnp.int32, (channels, rows_here), 1)
    wanted = (at_column // ROWS) * (2 * ROWS) + at_column % ROWS
    for part, which in ((same_half, my_half), (other_half, 1 - my_half)):
        pick = jnp.where(at_row == wanted + which * ROWS, 1.0, 0.0).astype(jnp.bfloat16)
        part[...] = jnp.dot(kept, pick, preferred_element_type=jnp.float32).astype(jnp.bfloat16)
    own_rows = prior[my_pair, my_half]
    at_row = lax.broadcasted_iota(jnp.int32, (ROWS, channels), 0)
    at_column = lax.broadcasted_iota(jnp.int32, (ROWS, channels), 1)
    diagonal = jnp.sum(
        jnp.where(at_column == at_row + me * ROWS, own_rows, 0.0), axis=1, keepdims=True
    )

    def tile_row(b):
        one = tiles_at[b // blocks_dev, pl.ds(b % blocks_dev, 1), :]
        return jnp.broadcast_to(one, (ROWS, LANES))

    def back_project(rows):
        parts = [
            jnp.dot(
                rows[b * ROWS:(b + 1) * ROWS], points[b // blocks_dev, b % blocks_dev],
                preferred_element_type=jnp.float32,
            )
            for b in range(blocks)
        ]
        rows_at = [tile_row(b) for b in range(blocks)]
        summed = []
        for t in range(tiles):
            one = jnp.where(rows_at[0] == t, parts[0], 0.0)
            for b in range(1, blocks):
                one = one + jnp.where(rows_at[b] == t, parts[b], 0.0)
            summed.append(one)
        return summed

    wait_bytes(rhs_got.at[pl.ds(0, group - 1)], setup_sems.at[1])
    wait_bytes(pre_got.at[pl.ds(0, group - 1)], setup_sems.at[3])
    if tm > 1:
        wait_bytes(tiles_at.at[pl.ds(0, tm - 1)], setup_sems.at[7])
        wait_bytes(points.at[pl.ds(0, tm - 1)], setup_sems.at[5])
    rhs_list = []
    for k in range(tm):
        span = rhs_got[k * dish]
        for j in range(1, dish):
            span = span + rhs_got[k * dish + j]
        rhs_list.append(span.reshape(span_rows, LANES))
    rhs = jnp.concatenate(rhs_list, axis=0).astype(jnp.bfloat16)
    for t, one in enumerate(back_project(rhs)):
        first = (t % tiles_own) * LANES
        scale = pre_got[t // tiles_own, :, first:first + LANES]
        pre[t] = scale
        state_r[t] = one
        state_u[t] = scale * one
    zero = jnp.zeros((tiles, ROWS, LANES), jnp.float32)
    state_x[...] = zero
    state_p[...] = zero
    tile_p[...] = jnp.zeros_like(tile_p)

    like_steps = [step for step in steps if step[2] % 2 == 0]
    sibling = lax.rem(my_dish + 1, 2)
    sibling_place = {
        "tm": my_tm, "freq": my_freq, "dish": my_dish - my_half + sibling,
    }

    def send_like(src, dst, send, recv):
        for step in like_steps:
            remote(src.at[lax.div(index_of(step), 2)], dst, send, recv, step).start()

    def send_dots(src, dst, send, recv):
        for step in steps:
            remote(src, dst.at[me], send, recv, step).start()
        dst[me] = src[...]

    def sum_of(dots):
        return jnp.sum(jnp.sum(dots[...], axis=0), axis=1, keepdims=True)

    def begin():
        u_send[...] = state_u[...].astype(jnp.bfloat16)
        send_like(u_send, field.at[my_half, my_pair], leg_sems.at[0], leg_sems.at[1])
        field[my_half, my_pair] = u_send[my_pair]
        first = jnp.sum(state_r[...] * state_u[...], axis=0)
        fresh_send[...] = jnp.sum(first, axis=0, keepdims=True)
        send_dots(fresh_send, fresh_got, leg_sems.at[8], leg_sems.at[9])

    def mix_all():
        wait_bytes(gain_got.at[pl.ds(0, group - 1)], setup_sems.at[9])
        wait_bytes(diags.at[pl.ds(0, dish - 1)], setup_sems.at[11])
        gain_list = []
        for j in range(dish):
            column = gain_got[j]
            for k in range(1, tm):
                column = column + gain_got[k * dish + j]
            gain_list.append(column)
        gain = jnp.concatenate(gain_list, axis=0)
        high, low = halves(gain * gain)
        weights = jnp.concatenate([high, low], axis=0).T.astype(jnp.bfloat16)

        def mix(k, carry):
            one = [diags[j, k] for j in range(dish)]
            stacked = jnp.concatenate(one + one, axis=0)
            mixing[k] = jnp.dot(weights, stacked, preferred_element_type=jnp.float32)
            return carry

        lax.fori_loop(0, DIAGS, mix, 0)

    def iteration(index, energy_old):
        wait_bytes(field.at[0, pl.ds(0, pairs - 1)], leg_sems.at[1])
        forward = pltpu.make_async_remote_copy(
            src_ref=field.at[my_half], dst_ref=field.at[my_half],
            send_sem=leg_sems.at[2], recv_sem=leg_sems.at[3],
            device_id=sibling_place, device_id_type=MESH,
        )
        forward.start()
        wait_bytes(fresh_got.at[pl.ds(0, devices - 1)], leg_sems.at[9])
        energy = sum_of(fresh_got)
        beta = jnp.where(index == 0, 0.0, energy / energy_old)
        state_p[...] = state_u[...] + beta[None] * state_p[...]
        for b in range(blocks):
            at = tile_row(b)
            seen = jnp.where(at == 0, state_p[0], 0.0)
            for t in range(1, tiles):
                seen = seen + jnp.where(at == t, state_p[t], 0.0)
            model[b * ROWS:(b + 1) * ROWS] = lax.dot_general(
                seen.astype(jnp.bfloat16), points[b // blocks_dev, b % blocks_dev],
                (((1,), (1,)), ((), ())), preferred_element_type=jnp.float32,
            ).astype(jnp.bfloat16).astype(jnp.float32)

        forward.wait()
        mine = field[my_half].reshape(rows_here, LANES).astype(jnp.float32)
        mine = mine + beta * tile_p[my_half]
        tile_p[my_half] = mine
        theirs = field[1 - my_half].reshape(rows_here, LANES).astype(jnp.float32)
        theirs = theirs + beta * tile_p[1 - my_half]
        tile_p[1 - my_half] = theirs
        applied = jnp.dot(
            same_half[...], mine.astype(jnp.bfloat16), preferred_element_type=jnp.float32
        ) + jnp.dot(
            other_half[...], theirs.astype(jnp.bfloat16), preferred_element_type=jnp.float32
        )
        back_send[...] = applied.reshape(pairs, ROWS, LANES).astype(jnp.bfloat16)
        send_like(back_send, back.at[my_pair], leg_sems.at[4], leg_sems.at[5])
        back[my_pair] = back_send[my_pair]

        tod = model[...]
        mixed = mixing[BAND] * tod
        for k in range(DIAGS):
            if k != BAND:
                mixed = mixed + mixing[k] * pltpu.roll(tod, (BAND - k) % LANES, 1)
        curve = jnp.zeros((ROWS, LANES), jnp.float32)
        for t, one in enumerate(back_project(mixed.astype(jnp.bfloat16))):
            here = state_p[t]
            term = one + diagonal * here
            state_w[t] = term
            curve = curve + here * term
        curve_send[...] = jnp.sum(curve, axis=0, keepdims=True) + jnp.sum(
            applied * mine, axis=0, keepdims=True
        )
        send_dots(curve_send, curve_got, leg_sems.at[6], leg_sems.at[7])
        wait_bytes(back.at[pl.ds(0, pairs - 1)], leg_sems.at[5])
        wait_bytes(curve_got.at[pl.ds(0, devices - 1)], leg_sems.at[7])
        length = energy / sum_of(curve_got)
        for t in range(tiles):
            operated = state_w[t] + back[t].astype(jnp.float32)
            state_x[t] = state_x[t] + length * state_p[t]
            residual = state_r[t] - length * operated
            state_r[t] = residual
            state_u[t] = pre[t] * residual
        wait_bytes(u_send.at[pl.ds(0, pairs - 1)], leg_sems.at[0])
        wait_bytes(back_send.at[pl.ds(0, pairs - 1)], leg_sems.at[4])
        wait_bytes(curve_got.at[pl.ds(0, devices - 1)], leg_sems.at[6])
        wait_bytes(fresh_got.at[pl.ds(0, devices - 1)], leg_sems.at[8])
        return energy

    def later(index, energy):
        begin()
        return iteration(index, energy)

    begin()
    mix_all()
    energy = iteration(0, jnp.ones((1, 1), jnp.float32))
    lax.fori_loop(1, ITERS, later, energy)

    for t in range(tiles):
        first = (t % tiles_own) * LANES
        end_send[t // tiles_own, 0, :, first:first + LANES] = state_x[t]
        end_send[t // tiles_own, 1, :, first:first + LANES] = state_r[t]
    for step in group_steps:
        t = tm_at[step[0]] * dish + dish_at[step[2]]
        remote(
            end_send.at[t], end_recv.at[member], setup_sems.at[12], setup_sems.at[13], step
        ).start()
    end_recv[member] = end_send[member]
    wait_bytes(rhs_send.at[pl.ds(0, group - 1)], setup_sems.at[0])
    wait_bytes(pre_got.at[pl.ds(0, group - 1)], setup_sems.at[2])
    for a in range(1, tm):
        wait_bytes(pointing, setup_sems.at[4])
        wait_bytes(tile_send, setup_sems.at[6])
    wait_bytes(gain_send.at[pl.ds(0, group - 1)], setup_sems.at[8])
    wait_bytes(diags.at[pl.ds(0, dish - 1)], setup_sems.at[10])
    wait_bytes(end_recv.at[pl.ds(0, group - 1)], setup_sems.at[13])
    for t in range(group):
        x_out[t * ROWS:(t + 1) * ROWS] = end_recv[t, 0]
        r_out[t * ROWS:(t + 1) * ROWS] = end_recv[t, 1]
    wait_bytes(end_send.at[pl.ds(0, group - 1)], setup_sems.at[12])


def local_body(time_data, pointing, coverage, noise_inv, gains, prior_inv, precond):
    tm, freq, dish = (lax.axis_size(name) for name in ("tm", "freq", "dish"))
    group = tm * dish
    devices = group * freq
    pairs = devices // 2
    dishes_dev, channels_dev, _ = time_data.shape
    channels = prior_inv.shape[0]
    blocks_dev = pointing.shape[0]
    tiles_own = precond.shape[1] // LANES
    tiles = tiles_own * group

    f32, bf16 = jnp.float32, jnp.bfloat16
    state = pltpu.VMEM((tiles, ROWS, LANES), f32)
    half = pltpu.VMEM((pairs * ROWS, pairs * ROWS), bf16)
    leg = pltpu.VMEM((pairs, ROWS, LANES), bf16)
    end = pltpu.VMEM((group, 2, ROWS, tiles_own * LANES), f32)
    rhs = pltpu.VMEM((group, blocks_dev, ROWS, LANES), f32)
    gain = pltpu.VMEM((group, dishes_dev, LANES), f32)
    dots = pltpu.VMEM((1, LANES), f32)
    all_dots = pltpu.VMEM((devices, 1, LANES), f32)
    vmem = pl.BlockSpec(memory_space=pltpu.VMEM)
    smem = pl.BlockSpec(memory_space=pltpu.SMEM)
    shape = jax.ShapeDtypeStruct(precond.shape, f32)
    return pl.pallas_call(
        functools.partial(kernel, (tm, freq, dish)),
        out_shape=(shape, shape),
        in_specs=[vmem, vmem, smem, vmem, vmem, vmem, vmem],
        out_specs=(vmem, vmem),
        scratch_shapes=[
            pltpu.VMEM((blocks_dev, LANES, channels_dev), f32),
            rhs, rhs, gain, gain,
            pltpu.VMEM((dishes_dev, 3 * BAND, LANES), f32),
            pltpu.VMEM((DIAGS, dishes_dev, LANES), bf16),
            pltpu.VMEM((dish, DIAGS, dishes_dev, LANES), bf16),
            pltpu.VMEM((tm,) + pointing.shape, bf16),
            pltpu.VMEM((8, LANES), jnp.int32),
            pltpu.VMEM((tm, 8, LANES), jnp.int32),
            pltpu.VMEM((group, ROWS, tiles_own * LANES), f32),
            pltpu.VMEM((DIAGS, LANES, LANES), f32),
            pltpu.VMEM((LANES, LANES), f32),
            state, state, state, state, state, state,
            pltpu.VMEM((2, pairs * ROWS, LANES), f32),
            half, half, leg,
            pltpu.VMEM((2, pairs, ROWS, LANES), bf16),
            leg, leg,
            dots, all_dots, dots, all_dots, end, end,
            pltpu.SemaphoreType.DMA((14,)),
            pltpu.SemaphoreType.DMA((10,)),
        ],
        compiler_params=pltpu.CompilerParams(
            collective_id=0, has_side_effects=True, vmem_limit_bytes=40 * 1024 * 1024
        ),
    )(
        time_data, pointing, coverage, noise_inv, gains.transpose(0, 2, 1),
        prior_inv.reshape(pairs, 2, ROWS, channels), precond,
    )


def body(time_data, pointing, coverage, noise_inv, gains, prior_inv, precond):
    group = lax.axis_size("tm") * lax.axis_size("dish")
    devices = group * lax.axis_size("freq")
    fits = (
        prior_inv.shape[0] == devices * ROWS
        and precond.shape[1] * group * 2 == devices * LANES
        and pointing.shape[0] * lax.axis_size("tm") * ROWS == LANES
        and time_data.shape[0] == ROWS
        and ROWS * lax.axis_size("dish") * 2 == LANES
        and time_data.shape[1] == LANES
    )
    run = local_body if fits else general_body
    return run(time_data, pointing, coverage, noise_inv, gains, prior_inv, precond)


def solution(mesh):
    return jax.shard_map(
        body,
        mesh=mesh,
        in_specs=(
            P("dish", "freq", "tm"),
            P("tm", None, None),
            P("tm"),
            P("dish", None, None),
            P("dish", "freq", "tm"),
            P(),
            P("freq", ("tm", "dish")),
        ),
        out_specs=(P("freq", ("tm", "dish")), P("freq", ("tm", "dish"))),
        check_vma=False,
    )
```

```python
import functools

import jax
import jax.numpy as jnp
from jax import lax
from jax.experimental import pallas as pl
from jax.experimental.pallas import tpu as pltpu
from jax.sharding import PartitionSpec as P

ITERS = 4
BAND = 16
DIAGS = 2 * BAND + 1
ROWS = 16
LANES = 128
MESH = pl.DeviceIdType.MESH


def shifted(block, axis, distance):
    devices = range(lax.axis_size(axis))
    route = [((i - distance) % len(devices), i) for i in devices]
    return lax.ppermute(block, axis, route)


def general_body(time_data, pointing, coverage, noise_inv, gains, prior_inv, precond):
    highest = lax.Precision.HIGHEST
    channels_dev = precond.shape[0]
    owned_pixels = precond.shape[1]
    blocks_dev = pointing.shape[0]
    dish_count = lax.axis_size("dish")
    owned_tiles = owned_pixels // 128
    region_tiles = owned_tiles * dish_count
    window_tiles = 2 * region_tiles
    tile_count = jnp.arange(owned_tiles, dtype=jnp.int32)
    first_owned = lax.axis_index("dish") * owned_tiles + tile_count
    wanted = jnp.concatenate([first_owned, first_owned + region_tiles])
    own_hot = (coverage[:, None] == wanted[None, :]).astype(jnp.float32)

    def collect(partial_tod):
        summed = lax.psum(partial_tod, "dish")
        tile_part = jnp.einsum(
            "cbt,bti->cbi",
            summed.astype(jnp.bfloat16),
            pointing,
            preferred_element_type=jnp.float32,
        )
        window = jnp.einsum("cbi,bw->cwi", tile_part, own_hot, precision=highest)
        own_part = window[:, :owned_tiles, :].reshape(channels_dev, owned_pixels)
        ahead_part = window[:, owned_tiles:, :].reshape(channels_dev, owned_pixels)
        arrived = shifted(ahead_part, "tm", 1)
        return own_part + arrived

    def energy_of(residual, scaled):
        return lax.psum(jnp.sum(residual * scaled), ("tm", "freq", "dish"))

    series = time_data.reshape(time_data.shape[0], channels_dev, blocks_dev, 128)
    rhs_weighted = jnp.einsum(
        "dcbs,dst->dcbt", series, noise_inv, preferred_element_type=jnp.float32
    )
    right_side = collect(jnp.sum(gains[:, :, :, None] * rhs_weighted, axis=0))
    estimate = jnp.zeros_like(right_side)
    residual = right_side
    scaled = precond * residual
    direction = scaled
    energy_now = energy_of(residual, scaled)
    for iteration in range(ITERS):
        swapped = lax.all_to_all(direction, "freq", split_axis=1, concat_axis=0, tiled=True)
        applied = jnp.dot(prior_inv, swapped, precision=highest, preferred_element_type=jnp.float32)
        region_map = lax.all_gather(direction.astype(jnp.bfloat16), "dish", axis=1, tiled=True)
        following = shifted(region_map, "tm", -1)
        data_window = jnp.concatenate([region_map, following], axis=1)
        tile_maps = data_window.reshape(channels_dev, window_tiles, 128)[:, coverage, :]
        model_tod = jnp.einsum(
            "cbp,bsp->cbs", tile_maps, pointing, preferred_element_type=jnp.float32
        ).astype(jnp.bfloat16)
        weighted = jnp.einsum(
            "cbs,dst->dcbt", model_tod, noise_inv, preferred_element_type=jnp.float32
        )
        mixed_part = jnp.sum((gains * gains)[:, :, :, None] * weighted, axis=0)
        operated = collect(mixed_part) + lax.all_to_all(
            applied, "freq", split_axis=0, concat_axis=1, tiled=True
        )
        curve_sum = lax.psum(jnp.sum(direction * operated), ("tm", "freq", "dish"))
        step_size = energy_now / curve_sum
        estimate = estimate + step_size * direction
        residual = residual - step_size * operated
        if iteration + 1 < ITERS:
            scaled = precond * residual
            energy_next = energy_of(residual, scaled)
            direction = scaled + energy_next / energy_now * direction
            energy_now = energy_next
    return (estimate, residual)


def halves(value):
    high = value.astype(jnp.bfloat16).astype(jnp.float32)
    return high, value - high


def total(value):
    return jnp.sum(jnp.sum(value, axis=0, keepdims=True), axis=1, keepdims=True)


def kernel(
    sizes, time_hbm, pointing_hbm, coverage, noise_hbm, gains_hbm, prior_hbm,
    precond_hbm, x_out, r_out, time_data, noise, gains, prior, precond, rhs_sum, rhs_send, rhs_got, gain_send, gain_got, diag_wide, diag_send, diags,
    points, turned_points, tile_send, tiles_at, pre_got, mixing, model, state_x, state_r, state_u,
    state_p, state_w, pre, tile_p, same_half, other_half, u_send, field, back_send,
    back, fresh_send, fresh_got, curve_send, curve_got, end_send, end_recv, load_sems, setup_sems, leg_sems,
):
    tm, freq, dish = sizes
    group = tm * dish
    devices = group * freq
    dishes_dev, channels_dev, _ = time_data.shape
    blocks_dev = pointing_hbm.shape[0]
    blocks = tm * blocks_dev
    span_rows = blocks_dev * ROWS
    tiles_own = precond.shape[1] // LANES
    tiles = tiles_own * group
    pairs = devices // 2
    my_tm = lax.axis_index("tm")
    my_freq = lax.axis_index("freq")
    my_dish = lax.axis_index("dish")
    member = my_tm * dish + my_dish
    me = my_freq * group + member
    my_pair = lax.div(me, 2)
    my_half = lax.rem(me, 2)

    tm_at = [lax.rem(my_tm + step, tm) for step in range(tm)]
    freq_at = [lax.rem(my_freq + step, freq) for step in range(freq)]
    dish_at = [lax.rem(my_dish + step, dish) for step in range(dish)]
    steps = [
        (a, b, c) for b in range(freq) for a in range(tm) for c in range(dish)
    ]
    steps = sorted(steps[1:], key=lambda s: (-min(s[1], freq - s[1]), s))

    def index_of(step):
        a, b, c = step
        return freq_at[b] * group + tm_at[a] * dish + dish_at[c]

    def place(step):
        a, b, c = step
        return {"tm": tm_at[a], "freq": freq_at[b], "dish": dish_at[c]}

    def remote(src, dst, send, recv, step):
        return pltpu.make_async_remote_copy(
            src_ref=src, dst_ref=dst, send_sem=send, recv_sem=recv,
            device_id=place(step), device_id_type=MESH,
        )

    def wait_bytes(ref, sem):
        pltpu.make_async_copy(ref, ref, sem).wait()

    loads = [
        pltpu.make_async_copy(src, dst, load_sems.at[i])
        for i, (src, dst) in enumerate(
            [
                (noise_hbm, noise), (gains_hbm, gains), (time_hbm, time_data),
                (pointing_hbm, points.at[my_tm]), (precond_hbm, precond), (prior_hbm, prior),
            ]
        )
    ]
    for load in loads:
        load.start()
    barrier = pltpu.get_barrier_semaphore()
    for step in steps:
        pl.semaphore_signal(barrier, inc=1, device_id=place(step), device_id_type=MESH)

    at_row = lax.broadcasted_iota(jnp.int32, (LANES, LANES), 0)
    at_column = lax.broadcasted_iota(jnp.int32, (LANES, LANES), 1)
    reverse = jnp.where(at_row + at_column == LANES - 1, 1.0, 0.0).astype(jnp.bfloat16)

    rhs_sum[...] = jnp.zeros_like(rhs_sum)
    for load in loads[:3]:
        load.wait()

    def dish_step(d, carry):
        weight = gains[d]
        for b in range(blocks_dev):
            series = time_data[d, :, b * LANES:(b + 1) * LANES]
            term = lax.dot_general(
                noise[d], series, (((1,), (1,)), ((), ())),
                preferred_element_type=jnp.float32,
            )
            rhs_sum[b] += weight[b:b + 1, :] * term
        upside = jnp.dot(reverse, noise[d], preferred_element_type=jnp.float32)
        skewed = pltpu.roll(upside, 1, 1, stride=1, stride_axis=0)
        turned = jnp.dot(
            skewed.T.astype(jnp.bfloat16), reverse, preferred_element_type=jnp.float32
        )
        diag_wide[d] = turned[0:2 * BAND]
        return carry

    lax.fori_loop(0, dishes_dev, dish_step, 0)
    for b in range(blocks_dev):
        rhs_send[:, b] = rhs_sum[b].T.reshape(group, ROWS, LANES)
    for k in range(BAND + 1):
        diag_send[k] = diag_wide[:, k, :].astype(jnp.bfloat16)
    lane = lax.broadcasted_iota(jnp.int32, (dishes_dev, LANES), 1)
    slot = [
        jnp.logical_and(
            lane >= my_tm * span_rows + b * ROWS, lane < my_tm * span_rows + (b + 1) * ROWS
        )
        for b in range(blocks_dev)
    ]
    for t in range(group):
        column = jnp.zeros((dishes_dev, LANES), jnp.float32)
        for b in range(blocks_dev):
            turn = lax.rem(my_tm * span_rows + (b * ROWS - t * ROWS + LANES), LANES)
            column = jnp.where(slot[b], pltpu.roll(gains[:, b, :], turn, 1), column)
        gain_send[t] = column
    row = lax.broadcasted_iota(jnp.int32, (8, LANES), 0)
    tile_rows = jnp.zeros((8, LANES), jnp.int32)
    for b in range(blocks_dev):
        tile = lax.rem(my_tm * (tiles // tm) + coverage[b], tiles)
        tile_rows = jnp.where(row == b, tile, tile_rows)
    tile_send[...] = tile_rows

    for load in loads[3:]:
        load.wait()
    pl.semaphore_wait(barrier, devices - 1)

    group_steps = [step for step in steps if step[1] == 0]
    for step in group_steps:
        t = tm_at[step[0]] * dish + dish_at[step[2]]
        remote(
            rhs_send.at[t], rhs_got.at[member], setup_sems.at[0], setup_sems.at[1], step
        ).start()
        remote(
            precond.at[pl.ds(pl.multiple_of(t * ROWS, ROWS), ROWS), :], pre_got.at[member],
            setup_sems.at[2], setup_sems.at[3], step,
        ).start()
    for a in range(1, tm):
        step = (a, 0, 0)
        remote(tile_send, tiles_at.at[my_tm], setup_sems.at[6], setup_sems.at[7], step).start()
        remote(
            points.at[my_tm], points.at[my_tm], setup_sems.at[4], setup_sems.at[5], step
        ).start()
    for step in group_steps:
        t = tm_at[step[0]] * dish + dish_at[step[2]]
        remote(
            gain_send.at[t], gain_got.at[member], setup_sems.at[8], setup_sems.at[9], step
        ).start()
    for c in range(1, dish):
        remote(
            diag_send, diags.at[my_dish], setup_sems.at[10], setup_sems.at[11], (0, 0, c)
        ).start()
    rhs_got[member] = rhs_send[member]
    pre_got[member] = precond[pl.ds(pl.multiple_of(member * ROWS, ROWS), ROWS), :]
    tiles_at[my_tm] = tile_send[...]
    gain_got[member] = gain_send[member]
    diags[my_dish] = diag_send[...]

    channels = devices * ROWS
    rows_here = pairs * ROWS
    kept = prior[:, my_half].reshape(rows_here, channels)
    at_row = lax.broadcasted_iota(jnp.int32, (rows_here, channels), 0)
    at_column = lax.broadcasted_iota(jnp.int32, (rows_here, channels), 1)
    channel = (at_row // ROWS) * (2 * ROWS) + my_half * ROWS + at_row % ROWS
    kept = jnp.where(channel == at_column, 0.0, kept).astype(jnp.bfloat16)
    at_row = lax.broadcasted_iota(jnp.int32, (channels, rows_here), 0)
    at_column = lax.broadcasted_iota(jnp.int32, (channels, rows_here), 1)
    wanted = (at_column // ROWS) * (2 * ROWS) + at_column % ROWS
    for part, which in ((same_half, my_half), (other_half, 1 - my_half)):
        pick = jnp.where(at_row == wanted + which * ROWS, 1.0, 0.0).astype(jnp.bfloat16)
        part[...] = jnp.dot(kept, pick, preferred_element_type=jnp.float32).astype(jnp.bfloat16)
    own_rows = prior[my_pair, my_half]
    at_row = lax.broadcasted_iota(jnp.int32, (ROWS, channels), 0)
    at_column = lax.broadcasted_iota(jnp.int32, (ROWS, channels), 1)
    diagonal = jnp.sum(
        jnp.where(at_column == at_row + me * ROWS, own_rows, 0.0), axis=1, keepdims=True
    )

    def tile_row(b):
        one = tiles_at[b // blocks_dev, pl.ds(b % blocks_dev, 1), :]
        return jnp.broadcast_to(one, (ROWS, LANES))

    def back_project(rows):
        parts = [
            jnp.dot(
                rows[b * ROWS:(b + 1) * ROWS], points[b // blocks_dev, b % blocks_dev],
                preferred_element_type=jnp.float32,
            )
            for b in range(blocks)
        ]
        rows_at = [tile_row(b) for b in range(blocks)]
        summed = []
        for t in range(tiles):
            one = jnp.where(rows_at[0] == t, parts[0], 0.0)
            for b in range(1, blocks):
                one = one + jnp.where(rows_at[b] == t, parts[b], 0.0)
            summed.append(one)
        return summed

    wait_bytes(rhs_got.at[pl.ds(0, group - 1)], setup_sems.at[1])
    wait_bytes(pre_got.at[pl.ds(0, group - 1)], setup_sems.at[3])
    if tm > 1:
        wait_bytes(tiles_at.at[pl.ds(0, tm - 1)], setup_sems.at[7])
        wait_bytes(points.at[pl.ds(0, tm - 1)], setup_sems.at[5])
    rhs_list = []
    for k in range(tm):
        span = rhs_got[k * dish]
        for j in range(1, dish):
            span = span + rhs_got[k * dish + j]
        rhs_list.append(span.reshape(span_rows, LANES))
    rhs = jnp.concatenate(rhs_list, axis=0).astype(jnp.bfloat16)
    for t, one in enumerate(back_project(rhs)):
        first = (t % tiles_own) * LANES
        scale = pre_got[t // tiles_own, :, first:first + LANES]
        pre[t] = scale
        state_r[t] = one
        state_u[t] = scale * one
    zero = jnp.zeros((tiles, ROWS, LANES), jnp.float32)
    state_x[...] = zero
    state_p[...] = zero
    tile_p[...] = jnp.zeros_like(tile_p)

    like_steps = [step for step in steps if step[2] % 2 == 0]
    sibling = lax.rem(my_dish + 1, 2)
    sibling_place = {
        "tm": my_tm, "freq": my_freq, "dish": my_dish - my_half + sibling,
    }

    def send_like(src, dst, send, recv):
        for step in like_steps:
            remote(src.at[lax.div(index_of(step), 2)], dst, send, recv, step).start()

    def send_dots(src, dst, send, recv):
        for step in steps:
            remote(src, dst.at[me], send, recv, step).start()
        dst[me] = src[...]

    def sum_of(dots):
        return jnp.sum(jnp.sum(dots[...], axis=0), axis=1, keepdims=True)

    def begin():
        u_send[...] = state_u[...].astype(jnp.bfloat16)
        send_like(u_send, field.at[my_half, my_pair], leg_sems.at[0], leg_sems.at[1])
        field[my_half, my_pair] = u_send[my_pair]
        first = jnp.sum(state_r[...] * state_u[...], axis=0)
        fresh_send[...] = jnp.sum(first, axis=0, keepdims=True)
        send_dots(fresh_send, fresh_got, leg_sems.at[8], leg_sems.at[9])

    def mix_all():
        for b in range(blocks):
            one = points[b // blocks_dev, b % blocks_dev].astype(jnp.float32)
            turned_points[b] = one.T.astype(jnp.bfloat16)
        wait_bytes(gain_got.at[pl.ds(0, group - 1)], setup_sems.at[9])
        wait_bytes(diags.at[pl.ds(0, dish - 1)], setup_sems.at[11])
        gain_list = []
        for j in range(dish):
            column = gain_got[j]
            for k in range(1, tm):
                column = column + gain_got[k * dish + j]
            gain_list.append(column)
        gain = jnp.concatenate(gain_list, axis=0)
        high, low = halves(gain * gain)
        weights = jnp.concatenate([high, low], axis=0).T.astype(jnp.bfloat16)

        def mix(k, carry):
            one = [diags[j, k] for j in range(dish)]
            stacked = jnp.concatenate(one + one, axis=0)
            one = jnp.dot(weights, stacked, preferred_element_type=jnp.float32)
            mixing[BAND + k] = one
            mixing[BAND - k] = pltpu.roll(one, k, 1)
            return carry

        lax.fori_loop(0, BAND + 1, mix, 0)

    def iteration(index, energy_old):
        wait_bytes(field.at[0, pl.ds(0, pairs - 1)], leg_sems.at[1])
        forward = pltpu.make_async_remote_copy(
            src_ref=field.at[my_half], dst_ref=field.at[my_half],
            send_sem=leg_sems.at[2], recv_sem=leg_sems.at[3],
            device_id=sibling_place, device_id_type=MESH,
        )
        forward.start()
        wait_bytes(fresh_got.at[pl.ds(0, devices - 1)], leg_sems.at[9])
        energy = sum_of(fresh_got)
        beta = jnp.where(index == 0, 0.0, energy / energy_old)
        state_p[...] = state_u[...] + beta[None] * state_p[...]
        for b in range(blocks):
            at = tile_row(b)
            seen = jnp.where(at == 0, state_p[0], 0.0)
            for t in range(1, tiles):
                seen = seen + jnp.where(at == t, state_p[t], 0.0)
            model[b * ROWS:(b + 1) * ROWS] = jnp.dot(
                seen.astype(jnp.bfloat16), turned_points[b],
                preferred_element_type=jnp.float32,
            ).astype(jnp.bfloat16).astype(jnp.float32)

        forward.wait()
        mine = field[my_half].reshape(rows_here, LANES).astype(jnp.float32)
        mine = mine + beta * tile_p[my_half]
        tile_p[my_half] = mine
        theirs = field[1 - my_half].reshape(rows_here, LANES).astype(jnp.float32)
        theirs = theirs + beta * tile_p[1 - my_half]
        tile_p[1 - my_half] = theirs
        applied = jnp.dot(
            same_half[...], mine.astype(jnp.bfloat16), preferred_element_type=jnp.float32
        ) + jnp.dot(
            other_half[...], theirs.astype(jnp.bfloat16), preferred_element_type=jnp.float32
        )
        back_send[...] = applied.reshape(pairs, ROWS, LANES).astype(jnp.bfloat16)
        send_like(back_send, back.at[my_pair], leg_sems.at[4], leg_sems.at[5])
        back[my_pair] = back_send[my_pair]

        tod = model[...]
        mixed = mixing[BAND] * tod
        for k in range(DIAGS):
            if k != BAND:
                mixed = mixed + mixing[k] * pltpu.roll(tod, (BAND - k) % LANES, 1)
        curve = jnp.zeros((ROWS, LANES), jnp.float32)
        for t, one in enumerate(back_project(mixed.astype(jnp.bfloat16))):
            here = state_p[t]
            term = one + diagonal * here
            state_w[t] = term
            curve = curve + here * term
        curve_send[...] = jnp.sum(curve, axis=0, keepdims=True) + jnp.sum(
            applied * mine, axis=0, keepdims=True
        )
        send_dots(curve_send, curve_got, leg_sems.at[6], leg_sems.at[7])
        wait_bytes(back.at[pl.ds(0, pairs - 1)], leg_sems.at[5])
        wait_bytes(curve_got.at[pl.ds(0, devices - 1)], leg_sems.at[7])
        length = energy / sum_of(curve_got)
        for t in range(tiles):
            operated = state_w[t] + back[t].astype(jnp.float32)
            state_x[t] = state_x[t] + length * state_p[t]
            residual = state_r[t] - length * operated
            state_r[t] = residual
            state_u[t] = pre[t] * residual
        wait_bytes(u_send.at[pl.ds(0, pairs - 1)], leg_sems.at[0])
        wait_bytes(back_send.at[pl.ds(0, pairs - 1)], leg_sems.at[4])
        wait_bytes(curve_got.at[pl.ds(0, devices - 1)], leg_sems.at[6])
        wait_bytes(fresh_got.at[pl.ds(0, devices - 1)], leg_sems.at[8])
        return energy

    def later(index, energy):
        begin()
        return iteration(index, energy)

    begin()
    mix_all()
    energy = iteration(0, jnp.ones((1, 1), jnp.float32))
    lax.fori_loop(1, ITERS, later, energy)

    for t in range(tiles):
        first = (t % tiles_own) * LANES
        end_send[t // tiles_own, 0, :, first:first + LANES] = state_x[t]
        end_send[t // tiles_own, 1, :, first:first + LANES] = state_r[t]
    for step in group_steps:
        t = tm_at[step[0]] * dish + dish_at[step[2]]
        remote(
            end_send.at[t], end_recv.at[member], setup_sems.at[12], setup_sems.at[13], step
        ).start()
    end_recv[member] = end_send[member]
    wait_bytes(rhs_send.at[pl.ds(0, group - 1)], setup_sems.at[0])
    wait_bytes(pre_got.at[pl.ds(0, group - 1)], setup_sems.at[2])
    for a in range(1, tm):
        wait_bytes(points.at[0], setup_sems.at[4])
        wait_bytes(tile_send, setup_sems.at[6])
    wait_bytes(gain_send.at[pl.ds(0, group - 1)], setup_sems.at[8])
    wait_bytes(diags.at[pl.ds(0, dish - 1)], setup_sems.at[10])
    wait_bytes(end_recv.at[pl.ds(0, group - 1)], setup_sems.at[13])
    for t in range(group):
        x_out[t * ROWS:(t + 1) * ROWS] = end_recv[t, 0]
        r_out[t * ROWS:(t + 1) * ROWS] = end_recv[t, 1]
    wait_bytes(end_send.at[pl.ds(0, group - 1)], setup_sems.at[12])


def local_body(time_data, pointing, coverage, noise_inv, gains, prior_inv, precond):
    tm, freq, dish = (lax.axis_size(name) for name in ("tm", "freq", "dish"))
    group = tm * dish
    devices = group * freq
    pairs = devices // 2
    dishes_dev, channels_dev, _ = time_data.shape
    channels = prior_inv.shape[0]
    blocks_dev = pointing.shape[0]
    tiles_own = precond.shape[1] // LANES
    tiles = tiles_own * group

    f32, bf16 = jnp.float32, jnp.bfloat16
    state = pltpu.VMEM((tiles, ROWS, LANES), f32)
    half = pltpu.VMEM((pairs * ROWS, pairs * ROWS), bf16)
    leg = pltpu.VMEM((pairs, ROWS, LANES), bf16)
    end = pltpu.VMEM((group, 2, ROWS, tiles_own * LANES), f32)
    rhs = pltpu.VMEM((group, blocks_dev, ROWS, LANES), f32)
    gain = pltpu.VMEM((group, dishes_dev, LANES), f32)
    dots = pltpu.VMEM((1, LANES), f32)
    all_dots = pltpu.VMEM((devices, 1, LANES), f32)
    vmem = pl.BlockSpec(memory_space=pltpu.VMEM)
    hbm = pl.BlockSpec(memory_space=pl.ANY)
    smem = pl.BlockSpec(memory_space=pltpu.SMEM)
    shape = jax.ShapeDtypeStruct(precond.shape, f32)
    return pl.pallas_call(
        functools.partial(kernel, (tm, freq, dish)),
        out_shape=(shape, shape),
        in_specs=[hbm, hbm, smem, hbm, hbm, hbm, hbm],
        out_specs=(vmem, vmem),
        scratch_shapes=[
            pltpu.VMEM(time_data.shape, bf16),
            pltpu.VMEM(noise_inv.shape, bf16),
            pltpu.VMEM((dishes_dev, blocks_dev, channels_dev), f32),
            pltpu.VMEM((pairs, 2, ROWS, channels), f32),
            pltpu.VMEM(precond.shape, f32),
            pltpu.VMEM((blocks_dev, LANES, channels_dev), f32),
            rhs, rhs, gain, gain,
            pltpu.VMEM((dishes_dev, 2 * BAND, LANES), f32),
            pltpu.VMEM((BAND + 1, dishes_dev, LANES), bf16),
            pltpu.VMEM((dish, BAND + 1, dishes_dev, LANES), bf16),
            pltpu.VMEM((tm,) + pointing.shape, bf16),
            pltpu.VMEM((tm * blocks_dev, LANES, LANES), bf16),
            pltpu.VMEM((8, LANES), jnp.int32),
            pltpu.VMEM((tm, 8, LANES), jnp.int32),
            pltpu.VMEM((group, ROWS, tiles_own * LANES), f32),
            pltpu.VMEM((DIAGS, LANES, LANES), f32),
            pltpu.VMEM((LANES, LANES), f32),
            state, state, state, state, state, state,
            pltpu.VMEM((2, pairs * ROWS, LANES), f32),
            half, half, leg,
            pltpu.VMEM((2, pairs, ROWS, LANES), bf16),
            leg, leg,
            dots, all_dots, dots, all_dots, end, end,
            pltpu.SemaphoreType.DMA((6,)),
            pltpu.SemaphoreType.DMA((14,)),
            pltpu.SemaphoreType.DMA((10,)),
        ],
        compiler_params=pltpu.CompilerParams(
            collective_id=0, has_side_effects=True, vmem_limit_bytes=60 * 1024 * 1024
        ),
    )(
        time_data, pointing, coverage, noise_inv, gains.transpose(0, 2, 1),
        prior_inv.reshape(pairs, 2, ROWS, channels), precond,
    )


def body(time_data, pointing, coverage, noise_inv, gains, prior_inv, precond):
    group = lax.axis_size("tm") * lax.axis_size("dish")
    devices = group * lax.axis_size("freq")
    fits = (
        prior_inv.shape[0] == devices * ROWS
        and precond.shape[1] * group * 2 == devices * LANES
        and pointing.shape[0] * lax.axis_size("tm") * ROWS == LANES
        and time_data.shape[0] == ROWS
        and ROWS * lax.axis_size("dish") * 2 == LANES
        and time_data.shape[1] == LANES
    )
    run = local_body if fits else general_body
    return run(time_data, pointing, coverage, noise_inv, gains, prior_inv, precond)


def solution(mesh):
    return jax.shard_map(
        body,
        mesh=mesh,
        in_specs=(
            P("dish", "freq", "tm"),
            P("tm", None, None),
            P("tm"),
            P("dish", None, None),
            P("dish", "freq", "tm"),
            P(),
            P("freq", ("tm", "dish")),
        ),
        out_specs=(P("freq", ("tm", "dish")), P("freq", ("tm", "dish"))),
        check_vma=False,
    )
```

```python
import functools

import jax
import jax.numpy as jnp
from jax import lax
from jax.experimental import pallas as pl
from jax.experimental.pallas import tpu as pltpu
from jax.sharding import PartitionSpec as P

ITERS = 4
BAND = 16
DIAGS = 2 * BAND + 1
ROWS = 16
LANES = 128
MESH = pl.DeviceIdType.MESH


def shifted(block, axis, distance):
    devices = range(lax.axis_size(axis))
    route = [((i - distance) % len(devices), i) for i in devices]
    return lax.ppermute(block, axis, route)


def general_body(time_data, pointing, coverage, noise_inv, gains, prior_inv, precond):
    highest = lax.Precision.HIGHEST
    channels_dev = precond.shape[0]
    owned_pixels = precond.shape[1]
    blocks_dev = pointing.shape[0]
    dish_count = lax.axis_size("dish")
    owned_tiles = owned_pixels // 128
    region_tiles = owned_tiles * dish_count
    window_tiles = 2 * region_tiles
    tile_count = jnp.arange(owned_tiles, dtype=jnp.int32)
    first_owned = lax.axis_index("dish") * owned_tiles + tile_count
    wanted = jnp.concatenate([first_owned, first_owned + region_tiles])
    own_hot = (coverage[:, None] == wanted[None, :]).astype(jnp.float32)

    def collect(partial_tod):
        summed = lax.psum(partial_tod, "dish")
        tile_part = jnp.einsum(
            "cbt,bti->cbi",
            summed.astype(jnp.bfloat16),
            pointing,
            preferred_element_type=jnp.float32,
        )
        window = jnp.einsum("cbi,bw->cwi", tile_part, own_hot, precision=highest)
        own_part = window[:, :owned_tiles, :].reshape(channels_dev, owned_pixels)
        ahead_part = window[:, owned_tiles:, :].reshape(channels_dev, owned_pixels)
        arrived = shifted(ahead_part, "tm", 1)
        return own_part + arrived

    def energy_of(residual, scaled):
        return lax.psum(jnp.sum(residual * scaled), ("tm", "freq", "dish"))

    series = time_data.reshape(time_data.shape[0], channels_dev, blocks_dev, 128)
    rhs_weighted = jnp.einsum(
        "dcbs,dst->dcbt", series, noise_inv, preferred_element_type=jnp.float32
    )
    right_side = collect(jnp.sum(gains[:, :, :, None] * rhs_weighted, axis=0))
    estimate = jnp.zeros_like(right_side)
    residual = right_side
    scaled = precond * residual
    direction = scaled
    energy_now = energy_of(residual, scaled)
    for iteration in range(ITERS):
        swapped = lax.all_to_all(direction, "freq", split_axis=1, concat_axis=0, tiled=True)
        applied = jnp.dot(prior_inv, swapped, precision=highest, preferred_element_type=jnp.float32)
        region_map = lax.all_gather(direction.astype(jnp.bfloat16), "dish", axis=1, tiled=True)
        following = shifted(region_map, "tm", -1)
        data_window = jnp.concatenate([region_map, following], axis=1)
        tile_maps = data_window.reshape(channels_dev, window_tiles, 128)[:, coverage, :]
        model_tod = jnp.einsum(
            "cbp,bsp->cbs", tile_maps, pointing, preferred_element_type=jnp.float32
        ).astype(jnp.bfloat16)
        weighted = jnp.einsum(
            "cbs,dst->dcbt", model_tod, noise_inv, preferred_element_type=jnp.float32
        )
        mixed_part = jnp.sum((gains * gains)[:, :, :, None] * weighted, axis=0)
        operated = collect(mixed_part) + lax.all_to_all(
            applied, "freq", split_axis=0, concat_axis=1, tiled=True
        )
        curve_sum = lax.psum(jnp.sum(direction * operated), ("tm", "freq", "dish"))
        step_size = energy_now / curve_sum
        estimate = estimate + step_size * direction
        residual = residual - step_size * operated
        if iteration + 1 < ITERS:
            scaled = precond * residual
            energy_next = energy_of(residual, scaled)
            direction = scaled + energy_next / energy_now * direction
            energy_now = energy_next
    return (estimate, residual)


def halves(value):
    high = value.astype(jnp.bfloat16).astype(jnp.float32)
    return high, value - high


def total(value):
    return jnp.sum(jnp.sum(value, axis=0, keepdims=True), axis=1, keepdims=True)


def kernel(
    sizes, time_hbm, pointing_hbm, coverage, noise_hbm, gains_hbm, prior_hbm,
    precond_hbm, end_recv, time_data, noise, gains, prior, precond, rhs_sum, rhs_send, rhs_got, gain_send, gain_got, diag_wide, diag_send, diags,
    points, turned_points, tile_send, tiles_at, pre_got, mixing, model, state_x, state_r, state_u,
    state_p, state_w, pre, tile_p, same_half, other_half, u_send, field, back_send,
    back, fresh_send, fresh_got, curve_send, curve_got, end_send, load_sems, setup_sems, leg_sems,
):
    tm, freq, dish = sizes
    group = tm * dish
    devices = group * freq
    dishes_dev, channels_dev, _ = time_data.shape
    blocks_dev = pointing_hbm.shape[0]
    blocks = tm * blocks_dev
    span_rows = blocks_dev * ROWS
    tiles_own = precond.shape[1] // LANES
    tiles = tiles_own * group
    pairs = devices // 2
    my_tm = lax.axis_index("tm")
    my_freq = lax.axis_index("freq")
    my_dish = lax.axis_index("dish")
    member = my_tm * dish + my_dish
    me = my_freq * group + member
    my_pair = lax.div(me, 2)
    my_half = lax.rem(me, 2)

    tm_at = [lax.rem(my_tm + step, tm) for step in range(tm)]
    freq_at = [lax.rem(my_freq + step, freq) for step in range(freq)]
    dish_at = [lax.rem(my_dish + step, dish) for step in range(dish)]
    steps = [
        (a, b, c) for b in range(freq) for a in range(tm) for c in range(dish)
    ]
    steps = sorted(steps[1:], key=lambda s: (-min(s[1], freq - s[1]), s))

    def index_of(step):
        a, b, c = step
        return freq_at[b] * group + tm_at[a] * dish + dish_at[c]

    def place(step):
        a, b, c = step
        return {"tm": tm_at[a], "freq": freq_at[b], "dish": dish_at[c]}

    def remote(src, dst, send, recv, step):
        return pltpu.make_async_remote_copy(
            src_ref=src, dst_ref=dst, send_sem=send, recv_sem=recv,
            device_id=place(step), device_id_type=MESH,
        )

    def wait_bytes(ref, sem):
        pltpu.make_async_copy(ref, ref, sem).wait()

    loads = [
        pltpu.make_async_copy(src, dst, load_sems.at[i])
        for i, (src, dst) in enumerate(
            [
                (noise_hbm, noise), (gains_hbm, gains), (time_hbm, time_data),
                (pointing_hbm, points.at[my_tm]), (precond_hbm, precond), (prior_hbm, prior),
            ]
        )
    ]
    for load in loads:
        load.start()
    barrier = pltpu.get_barrier_semaphore()
    for step in steps:
        pl.semaphore_signal(barrier, inc=1, device_id=place(step), device_id_type=MESH)

    at_row = lax.broadcasted_iota(jnp.int32, (LANES, LANES), 0)
    at_column = lax.broadcasted_iota(jnp.int32, (LANES, LANES), 1)
    reverse = jnp.where(at_row + at_column == LANES - 1, 1.0, 0.0).astype(jnp.bfloat16)

    rhs_sum[...] = jnp.zeros_like(rhs_sum)
    for load in loads[:3]:
        load.wait()

    def dish_step(d, carry):
        weight = gains[d]
        for b in range(blocks_dev):
            series = time_data[d, :, b * LANES:(b + 1) * LANES]
            term = lax.dot_general(
                noise[d], series, (((1,), (1,)), ((), ())),
                preferred_element_type=jnp.float32,
            )
            rhs_sum[b] += weight[b:b + 1, :] * term
        return carry

    def diagonal_step(d, carry):
        upside = jnp.dot(reverse, noise[d], preferred_element_type=jnp.float32)
        skewed = pltpu.roll(upside, 1, 1, stride=1, stride_axis=0)
        turned = jnp.dot(
            skewed.T[0:2 * BAND].astype(jnp.bfloat16), reverse,
            preferred_element_type=jnp.float32,
        )
        diag_wide[d] = turned
        return carry

    group_steps = [step for step in steps if step[1] == 0]
    members = [tm_at[step[0]] * dish + dish_at[step[2]] for step in group_steps]
    row = lax.broadcasted_iota(jnp.int32, (8, LANES), 0)
    tile_rows = jnp.zeros((8, LANES), jnp.int32)
    for b in range(blocks_dev):
        tile = lax.rem(my_tm * (tiles // tm) + coverage[b], tiles)
        tile_rows = jnp.where(row == b, tile, tile_rows)
    tile_send[...] = tile_rows

    lax.fori_loop(0, dishes_dev // 2, dish_step, 0, unroll=4)
    for load in loads[3:]:
        load.wait()
    pl.semaphore_wait(barrier, devices - 1)
    for a in range(1, tm):
        step = (a, 0, 0)
        remote(tile_send, tiles_at.at[my_tm], setup_sems.at[6], setup_sems.at[7], step).start()
        remote(
            points.at[my_tm], points.at[my_tm], setup_sems.at[4], setup_sems.at[5], step
        ).start()
    for step, t in zip(group_steps, members):
        remote(
            precond.at[pl.ds(pl.multiple_of(t * ROWS, ROWS), ROWS), :], pre_got.at[member],
            setup_sems.at[2], setup_sems.at[3], step,
        ).start()
    lax.fori_loop(dishes_dev // 2, dishes_dev, dish_step, 0, unroll=4)
    for b in range(blocks_dev):
        rhs_send[:, b] = rhs_sum[b].T.reshape(group, ROWS, LANES)
    for step, t in zip(group_steps, members):
        remote(
            rhs_send.at[t], rhs_got.at[member], setup_sems.at[0], setup_sems.at[1], step
        ).start()

    lax.fori_loop(0, dishes_dev, diagonal_step, 0, unroll=4)
    for k in range(BAND + 1):
        diag_send[k] = diag_wide[:, k, :].astype(jnp.bfloat16)
    for c in range(1, dish):
        remote(
            diag_send, diags.at[my_dish], setup_sems.at[10], setup_sems.at[11], (0, 0, c)
        ).start()
    lane = lax.broadcasted_iota(jnp.int32, (dishes_dev, LANES), 1)
    slot = [
        jnp.logical_and(
            lane >= my_tm * span_rows + b * ROWS, lane < my_tm * span_rows + (b + 1) * ROWS
        )
        for b in range(blocks_dev)
    ]
    for t in range(group):
        column = jnp.zeros((dishes_dev, LANES), jnp.float32)
        for b in range(blocks_dev):
            turn = lax.rem(my_tm * span_rows + (b * ROWS - t * ROWS + LANES), LANES)
            column = jnp.where(slot[b], pltpu.roll(gains[:, b, :], turn, 1), column)
        gain_send[t] = column
    for step in group_steps:
        t = tm_at[step[0]] * dish + dish_at[step[2]]
        remote(
            gain_send.at[t], gain_got.at[member], setup_sems.at[8], setup_sems.at[9], step
        ).start()
    rhs_got[member] = rhs_send[member]
    pre_got[member] = precond[pl.ds(pl.multiple_of(member * ROWS, ROWS), ROWS), :]
    tiles_at[my_tm] = tile_send[...]
    gain_got[member] = gain_send[member]
    diags[my_dish] = diag_send[...]

    channels = devices * ROWS
    rows_here = pairs * ROWS
    kept = prior[:, my_half].reshape(rows_here, channels)
    at_row = lax.broadcasted_iota(jnp.int32, (rows_here, channels), 0)
    at_column = lax.broadcasted_iota(jnp.int32, (rows_here, channels), 1)
    channel = (at_row // ROWS) * (2 * ROWS) + my_half * ROWS + at_row % ROWS
    kept = jnp.where(channel == at_column, 0.0, kept).astype(jnp.bfloat16)
    at_row = lax.broadcasted_iota(jnp.int32, (channels, rows_here), 0)
    at_column = lax.broadcasted_iota(jnp.int32, (channels, rows_here), 1)
    wanted = (at_column // ROWS) * (2 * ROWS) + at_column % ROWS
    for part, which in ((same_half, my_half), (other_half, 1 - my_half)):
        pick = jnp.where(at_row == wanted + which * ROWS, 1.0, 0.0).astype(jnp.bfloat16)
        part[...] = jnp.dot(kept, pick, preferred_element_type=jnp.float32).astype(jnp.bfloat16)
    own_rows = prior[my_pair, my_half]
    at_row = lax.broadcasted_iota(jnp.int32, (ROWS, channels), 0)
    at_column = lax.broadcasted_iota(jnp.int32, (ROWS, channels), 1)
    diagonal = jnp.sum(
        jnp.where(at_column == at_row + me * ROWS, own_rows, 0.0), axis=1, keepdims=True
    )

    def tile_row(b):
        one = tiles_at[b // blocks_dev, pl.ds(b % blocks_dev, 1), :]
        return jnp.broadcast_to(one, (ROWS, LANES))

    def back_project(rows):
        parts = [
            jnp.dot(
                rows[b * ROWS:(b + 1) * ROWS], points[b // blocks_dev, b % blocks_dev],
                preferred_element_type=jnp.float32,
            )
            for b in range(blocks)
        ]
        rows_at = [tile_row(b) for b in range(blocks)]
        summed = []
        for t in range(tiles):
            one = jnp.where(rows_at[0] == t, parts[0], 0.0)
            for b in range(1, blocks):
                one = one + jnp.where(rows_at[b] == t, parts[b], 0.0)
            summed.append(one)
        return summed

    wait_bytes(rhs_got.at[pl.ds(0, group - 1)], setup_sems.at[1])
    wait_bytes(pre_got.at[pl.ds(0, group - 1)], setup_sems.at[3])
    if tm > 1:
        wait_bytes(tiles_at.at[pl.ds(0, tm - 1)], setup_sems.at[7])
        wait_bytes(points.at[pl.ds(0, tm - 1)], setup_sems.at[5])
    rhs_list = []
    for k in range(tm):
        span = rhs_got[k * dish]
        for j in range(1, dish):
            span = span + rhs_got[k * dish + j]
        rhs_list.append(span.reshape(span_rows, LANES))
    rhs = jnp.concatenate(rhs_list, axis=0).astype(jnp.bfloat16)
    for t, one in enumerate(back_project(rhs)):
        first = (t % tiles_own) * LANES
        scale = pre_got[t // tiles_own, :, first:first + LANES]
        pre[t] = scale
        state_r[t] = one
        state_u[t] = scale * one
    zero = jnp.zeros((tiles, ROWS, LANES), jnp.float32)
    state_x[...] = zero
    state_p[...] = zero
    tile_p[...] = jnp.zeros_like(tile_p)

    like_steps = [step for step in steps if step[2] % 2 == 0]
    sibling = lax.rem(my_dish + 1, 2)
    sibling_place = {
        "tm": my_tm, "freq": my_freq, "dish": my_dish - my_half + sibling,
    }

    def send_like(src, dst, send, recv):
        for step in like_steps:
            remote(src.at[lax.div(index_of(step), 2)], dst, send, recv, step).start()

    def send_dots(src, dst, send, recv):
        for step in steps:
            remote(src, dst.at[me], send, recv, step).start()
        dst[me] = src[...]

    def sum_of(dots):
        return jnp.sum(jnp.sum(dots[...], axis=0), axis=1, keepdims=True)

    def begin():
        u_send[...] = state_u[...].astype(jnp.bfloat16)
        send_like(u_send, field.at[my_half, my_pair], leg_sems.at[0], leg_sems.at[1])
        field[my_half, my_pair] = u_send[my_pair]
        first = jnp.sum(state_r[...] * state_u[...], axis=0)
        fresh_send[...] = jnp.sum(first, axis=0, keepdims=True)
        send_dots(fresh_send, fresh_got, leg_sems.at[8], leg_sems.at[9])

    def mix_all():
        for b in range(blocks):
            one = points[b // blocks_dev, b % blocks_dev].astype(jnp.float32)
            turned_points[b] = one.T.astype(jnp.bfloat16)
        wait_bytes(gain_got.at[pl.ds(0, group - 1)], setup_sems.at[9])
        wait_bytes(diags.at[pl.ds(0, dish - 1)], setup_sems.at[11])
        gain_list = []
        for j in range(dish):
            column = gain_got[j]
            for k in range(1, tm):
                column = column + gain_got[k * dish + j]
            gain_list.append(column)
        gain = jnp.concatenate(gain_list, axis=0)
        high, low = halves(gain * gain)
        weights = jnp.concatenate([high, low], axis=0).T.astype(jnp.bfloat16)

        for k in range(BAND + 1):
            one = [diags[j, k] for j in range(dish)]
            stacked = jnp.concatenate(one + one, axis=0)
            one = jnp.dot(weights, stacked, preferred_element_type=jnp.float32)
            mixing[BAND + k] = one
            if k > 0:
                mixing[BAND - k] = pltpu.roll(one, k, 1)

    def iteration(index, energy_old):
        wait_bytes(field.at[0, pl.ds(0, pairs - 1)], leg_sems.at[1])
        forward = pltpu.make_async_remote_copy(
            src_ref=field.at[my_half], dst_ref=field.at[my_half],
            send_sem=leg_sems.at[2], recv_sem=leg_sems.at[3],
            device_id=sibling_place, device_id_type=MESH,
        )
        forward.start()
        wait_bytes(fresh_got.at[pl.ds(0, devices - 1)], leg_sems.at[9])
        energy = sum_of(fresh_got)
        beta = jnp.where(index == 0, 0.0, energy / energy_old)
        state_p[...] = state_u[...] + beta[None] * state_p[...]
        for b in range(blocks):
            at = tile_row(b)
            seen = jnp.where(at == 0, state_p[0], 0.0)
            for t in range(1, tiles):
                seen = seen + jnp.where(at == t, state_p[t], 0.0)
            model[b * ROWS:(b + 1) * ROWS] = jnp.dot(
                seen.astype(jnp.bfloat16), turned_points[b],
                preferred_element_type=jnp.float32,
            ).astype(jnp.bfloat16).astype(jnp.float32)

        forward.wait()
        mine = field[my_half].reshape(rows_here, LANES).astype(jnp.float32)
        mine = mine + beta * tile_p[my_half]
        tile_p[my_half] = mine
        theirs = field[1 - my_half].reshape(rows_here, LANES).astype(jnp.float32)
        theirs = theirs + beta * tile_p[1 - my_half]
        tile_p[1 - my_half] = theirs
        applied = jnp.dot(
            same_half[...], mine.astype(jnp.bfloat16), preferred_element_type=jnp.float32
        ) + jnp.dot(
            other_half[...], theirs.astype(jnp.bfloat16), preferred_element_type=jnp.float32
        )
        back_send[...] = applied.reshape(pairs, ROWS, LANES).astype(jnp.bfloat16)
        send_like(back_send, back.at[my_pair], leg_sems.at[4], leg_sems.at[5])
        back[my_pair] = back_send[my_pair]

        tod = model[...]
        mixed = mixing[BAND] * tod
        for k in range(DIAGS):
            if k != BAND:
                mixed = mixed + mixing[k] * pltpu.roll(tod, (BAND - k) % LANES, 1)
        curve = jnp.zeros((ROWS, LANES), jnp.float32)
        for t, one in enumerate(back_project(mixed.astype(jnp.bfloat16))):
            here = state_p[t]
            term = one + diagonal * here
            state_w[t] = term
            curve = curve + here * term
        curve_send[...] = jnp.sum(curve, axis=0, keepdims=True) + jnp.sum(
            applied * mine, axis=0, keepdims=True
        )
        send_dots(curve_send, curve_got, leg_sems.at[6], leg_sems.at[7])
        wait_bytes(back.at[pl.ds(0, pairs - 1)], leg_sems.at[5])
        wait_bytes(curve_got.at[pl.ds(0, devices - 1)], leg_sems.at[7])
        length = energy / sum_of(curve_got)
        for t in range(tiles):
            operated = state_w[t] + back[t].astype(jnp.float32)
            state_x[t] = state_x[t] + length * state_p[t]
            residual = state_r[t] - length * operated
            state_r[t] = residual
            state_u[t] = pre[t] * residual
        wait_bytes(u_send.at[pl.ds(0, pairs - 1)], leg_sems.at[0])
        wait_bytes(back_send.at[pl.ds(0, pairs - 1)], leg_sems.at[4])
        wait_bytes(curve_got.at[pl.ds(0, devices - 1)], leg_sems.at[6])
        wait_bytes(fresh_got.at[pl.ds(0, devices - 1)], leg_sems.at[8])
        return energy

    def later(index, energy):
        begin()
        return iteration(index, energy)

    begin()
    mix_all()
    energy = iteration(0, jnp.ones((1, 1), jnp.float32))
    lax.fori_loop(1, ITERS, later, energy)

    for t in range(tiles):
        first = (t % tiles_own) * LANES
        end_send[t // tiles_own, 0, :, first:first + LANES] = state_x[t]
        end_send[t // tiles_own, 1, :, first:first + LANES] = state_r[t]
    for step in group_steps:
        t = tm_at[step[0]] * dish + dish_at[step[2]]
        remote(
            end_send.at[t], end_recv.at[member], setup_sems.at[12], setup_sems.at[13], step
        ).start()
    end_recv[member] = end_send[member]
    wait_bytes(rhs_send.at[pl.ds(0, group - 1)], setup_sems.at[0])
    wait_bytes(pre_got.at[pl.ds(0, group - 1)], setup_sems.at[2])
    for a in range(1, tm):
        wait_bytes(points.at[0], setup_sems.at[4])
        wait_bytes(tile_send, setup_sems.at[6])
    wait_bytes(gain_send.at[pl.ds(0, group - 1)], setup_sems.at[8])
    wait_bytes(diags.at[pl.ds(0, dish - 1)], setup_sems.at[10])
    wait_bytes(end_recv.at[pl.ds(0, group - 1)], setup_sems.at[13])
    wait_bytes(end_send.at[pl.ds(0, group - 1)], setup_sems.at[12])


def spread(ends, x_out, r_out):
    for t in range(ends.shape[0]):
        x_out[t * ROWS:(t + 1) * ROWS] = ends[t, 0]
        r_out[t * ROWS:(t + 1) * ROWS] = ends[t, 1]


def local_body(time_data, pointing, coverage, noise_inv, gains, prior_inv, precond):
    tm, freq, dish = (lax.axis_size(name) for name in ("tm", "freq", "dish"))
    group = tm * dish
    devices = group * freq
    pairs = devices // 2
    dishes_dev, channels_dev, _ = time_data.shape
    channels = prior_inv.shape[0]
    blocks_dev = pointing.shape[0]
    tiles_own = precond.shape[1] // LANES
    tiles = tiles_own * group

    f32, bf16 = jnp.float32, jnp.bfloat16
    state = pltpu.VMEM((tiles, ROWS, LANES), f32)
    half = pltpu.VMEM((pairs * ROWS, pairs * ROWS), bf16)
    leg = pltpu.VMEM((pairs, ROWS, LANES), bf16)
    end = pltpu.VMEM((group, 2, ROWS, tiles_own * LANES), f32)
    rhs = pltpu.VMEM((group, blocks_dev, ROWS, LANES), f32)
    gain = pltpu.VMEM((group, dishes_dev, LANES), f32)
    dots = pltpu.VMEM((1, LANES), f32)
    all_dots = pltpu.VMEM((devices, 1, LANES), f32)
    vmem = pl.BlockSpec(memory_space=pltpu.VMEM)
    hbm = pl.BlockSpec(memory_space=pl.ANY)
    smem = pl.BlockSpec(memory_space=pltpu.SMEM)
    shape = jax.ShapeDtypeStruct(precond.shape, f32)
    ends = pl.pallas_call(
        functools.partial(kernel, (tm, freq, dish)),
        out_shape=jax.ShapeDtypeStruct((group, 2, ROWS, tiles_own * LANES), f32),
        in_specs=[hbm, hbm, smem, hbm, hbm, hbm, hbm],
        out_specs=vmem,
        scratch_shapes=[
            pltpu.VMEM(time_data.shape, bf16),
            pltpu.VMEM(noise_inv.shape, bf16),
            pltpu.VMEM((dishes_dev, blocks_dev, channels_dev), f32),
            pltpu.VMEM((pairs, 2, ROWS, channels), f32),
            pltpu.VMEM(precond.shape, f32),
            pltpu.VMEM((blocks_dev, LANES, channels_dev), f32),
            rhs, rhs, gain, gain,
            pltpu.VMEM((dishes_dev, 2 * BAND, LANES), f32),
            pltpu.VMEM((BAND + 1, dishes_dev, LANES), bf16),
            pltpu.VMEM((dish, BAND + 1, dishes_dev, LANES), bf16),
            pltpu.VMEM((tm,) + pointing.shape, bf16),
            pltpu.VMEM((tm * blocks_dev, LANES, LANES), bf16),
            pltpu.VMEM((8, LANES), jnp.int32),
            pltpu.VMEM((tm, 8, LANES), jnp.int32),
            pltpu.VMEM((group, ROWS, tiles_own * LANES), f32),
            pltpu.VMEM((DIAGS, LANES, LANES), f32),
            pltpu.VMEM((LANES, LANES), f32),
            state, state, state, state, state, state,
            pltpu.VMEM((2, pairs * ROWS, LANES), f32),
            half, half, leg,
            pltpu.VMEM((2, pairs, ROWS, LANES), bf16),
            leg, leg,
            dots, all_dots, dots, all_dots, end,
            pltpu.SemaphoreType.DMA((6,)),
            pltpu.SemaphoreType.DMA((14,)),
            pltpu.SemaphoreType.DMA((10,)),
        ],
        compiler_params=pltpu.CompilerParams(
            collective_id=0, has_side_effects=True, vmem_limit_bytes=60 * 1024 * 1024
        ),
    )(
        time_data, pointing, coverage, noise_inv, gains.transpose(0, 2, 1),
        prior_inv.reshape(pairs, 2, ROWS, channels), precond,
    )
    return pl.pallas_call(
        spread, out_shape=(shape, shape), in_specs=[vmem], out_specs=(vmem, vmem)
    )(ends)


def body(time_data, pointing, coverage, noise_inv, gains, prior_inv, precond):
    group = lax.axis_size("tm") * lax.axis_size("dish")
    devices = group * lax.axis_size("freq")
    fits = (
        prior_inv.shape[0] == devices * ROWS
        and precond.shape[1] * group * 2 == devices * LANES
        and pointing.shape[0] * lax.axis_size("tm") * ROWS == LANES
        and time_data.shape[0] == ROWS
        and ROWS * lax.axis_size("dish") * 2 == LANES
        and time_data.shape[1] == LANES
    )
    run = local_body if fits else general_body
    return run(time_data, pointing, coverage, noise_inv, gains, prior_inv, precond)


def solution(mesh):
    return jax.shard_map(
        body,
        mesh=mesh,
        in_specs=(
            P("dish", "freq", "tm"),
            P("tm", None, None),
            P("tm"),
            P("dish", None, None),
            P("dish", "freq", "tm"),
            P(),
            P("freq", ("tm", "dish")),
        ),
        out_specs=(P("freq", ("tm", "dish")), P("freq", ("tm", "dish"))),
        check_vma=False,
    )
```

```python
import functools

import jax
import jax.numpy as jnp
from jax import lax
from jax.experimental import pallas as pl
from jax.experimental.pallas import tpu as pltpu
from jax.sharding import PartitionSpec as P

ITERS = 4
BAND = 16
DIAGS = 2 * BAND + 1
ROWS = 16
LANES = 128
MESH = pl.DeviceIdType.MESH


def shifted(block, axis, distance):
    devices = range(lax.axis_size(axis))
    route = [((i - distance) % len(devices), i) for i in devices]
    return lax.ppermute(block, axis, route)


def general_body(time_data, pointing, coverage, noise_inv, gains, prior_inv, precond):
    highest = lax.Precision.HIGHEST
    channels_dev = precond.shape[0]
    owned_pixels = precond.shape[1]
    blocks_dev = pointing.shape[0]
    dish_count = lax.axis_size("dish")
    owned_tiles = owned_pixels // 128
    region_tiles = owned_tiles * dish_count
    window_tiles = 2 * region_tiles
    tile_count = jnp.arange(owned_tiles, dtype=jnp.int32)
    first_owned = lax.axis_index("dish") * owned_tiles + tile_count
    wanted = jnp.concatenate([first_owned, first_owned + region_tiles])
    own_hot = (coverage[:, None] == wanted[None, :]).astype(jnp.float32)

    def collect(partial_tod):
        summed = lax.psum(partial_tod, "dish")
        tile_part = jnp.einsum(
            "cbt,bti->cbi",
            summed.astype(jnp.bfloat16),
            pointing,
            preferred_element_type=jnp.float32,
        )
        window = jnp.einsum("cbi,bw->cwi", tile_part, own_hot, precision=highest)
        own_part = window[:, :owned_tiles, :].reshape(channels_dev, owned_pixels)
        ahead_part = window[:, owned_tiles:, :].reshape(channels_dev, owned_pixels)
        arrived = shifted(ahead_part, "tm", 1)
        return own_part + arrived

    def energy_of(residual, scaled):
        return lax.psum(jnp.sum(residual * scaled), ("tm", "freq", "dish"))

    series = time_data.reshape(time_data.shape[0], channels_dev, blocks_dev, 128)
    rhs_weighted = jnp.einsum(
        "dcbs,dst->dcbt", series, noise_inv, preferred_element_type=jnp.float32
    )
    right_side = collect(jnp.sum(gains[:, :, :, None] * rhs_weighted, axis=0))
    estimate = jnp.zeros_like(right_side)
    residual = right_side
    scaled = precond * residual
    direction = scaled
    energy_now = energy_of(residual, scaled)
    for iteration in range(ITERS):
        swapped = lax.all_to_all(direction, "freq", split_axis=1, concat_axis=0, tiled=True)
        applied = jnp.dot(prior_inv, swapped, precision=highest, preferred_element_type=jnp.float32)
        region_map = lax.all_gather(direction.astype(jnp.bfloat16), "dish", axis=1, tiled=True)
        following = shifted(region_map, "tm", -1)
        data_window = jnp.concatenate([region_map, following], axis=1)
        tile_maps = data_window.reshape(channels_dev, window_tiles, 128)[:, coverage, :]
        model_tod = jnp.einsum(
            "cbp,bsp->cbs", tile_maps, pointing, preferred_element_type=jnp.float32
        ).astype(jnp.bfloat16)
        weighted = jnp.einsum(
            "cbs,dst->dcbt", model_tod, noise_inv, preferred_element_type=jnp.float32
        )
        mixed_part = jnp.sum((gains * gains)[:, :, :, None] * weighted, axis=0)
        operated = collect(mixed_part) + lax.all_to_all(
            applied, "freq", split_axis=0, concat_axis=1, tiled=True
        )
        curve_sum = lax.psum(jnp.sum(direction * operated), ("tm", "freq", "dish"))
        step_size = energy_now / curve_sum
        estimate = estimate + step_size * direction
        residual = residual - step_size * operated
        if iteration + 1 < ITERS:
            scaled = precond * residual
            energy_next = energy_of(residual, scaled)
            direction = scaled + energy_next / energy_now * direction
            energy_now = energy_next
    return (estimate, residual)


def halves(value):
    high = value.astype(jnp.bfloat16).astype(jnp.float32)
    return high, value - high


def total(value):
    return jnp.sum(jnp.sum(value, axis=0, keepdims=True), axis=1, keepdims=True)


def kernel(
    sizes, time_hbm, pointing_hbm, coverage, noise_hbm, gains_hbm, prior_hbm,
    precond_hbm, end_recv, time_data, noise, gains, prior, precond, rhs_sum, rhs_send, rhs_got, gain_send, gain_got, diag_wide, diag_send, diags,
    points, turned_points, tile_send, tiles_at, pre_got, mixing, model, state_x, state_r, state_u,
    state_p, state_w, pre, tile_p, same_half, other_half, u_send, field, back_send,
    back, fresh_send, fresh_got, curve_send, curve_got, early_send, early_got, end_send, load_sems, setup_sems, leg_sems,
):
    tm, freq, dish = sizes
    group = tm * dish
    devices = group * freq
    dishes_dev, channels_dev, _ = time_data.shape
    blocks_dev = pointing_hbm.shape[0]
    blocks = tm * blocks_dev
    span_rows = blocks_dev * ROWS
    tiles_own = precond.shape[1] // LANES
    tiles = tiles_own * group
    pairs = devices // 2
    my_tm = lax.axis_index("tm")
    my_freq = lax.axis_index("freq")
    my_dish = lax.axis_index("dish")
    member = my_tm * dish + my_dish
    me = my_freq * group + member
    my_pair = lax.div(me, 2)
    my_half = lax.rem(me, 2)

    tm_at = [lax.rem(my_tm + step, tm) for step in range(tm)]
    freq_at = [lax.rem(my_freq + step, freq) for step in range(freq)]
    dish_at = [lax.rem(my_dish + step, dish) for step in range(dish)]
    steps = [
        (a, b, c) for b in range(freq) for a in range(tm) for c in range(dish)
    ]
    steps = sorted(steps[1:], key=lambda s: (-min(s[1], freq - s[1]), s))

    def index_of(step):
        a, b, c = step
        return freq_at[b] * group + tm_at[a] * dish + dish_at[c]

    def place(step):
        a, b, c = step
        return {"tm": tm_at[a], "freq": freq_at[b], "dish": dish_at[c]}

    def remote(src, dst, send, recv, step):
        return pltpu.make_async_remote_copy(
            src_ref=src, dst_ref=dst, send_sem=send, recv_sem=recv,
            device_id=place(step), device_id_type=MESH,
        )

    def wait_bytes(ref, sem):
        pltpu.make_async_copy(ref, ref, sem).wait()

    loads = [
        pltpu.make_async_copy(src, dst, load_sems.at[i])
        for i, (src, dst) in enumerate(
            [
                (noise_hbm, noise), (gains_hbm, gains), (time_hbm, time_data),
                (pointing_hbm, points.at[my_tm]), (precond_hbm, precond), (prior_hbm, prior),
            ]
        )
    ]
    for load in loads:
        load.start()
    barrier = pltpu.get_barrier_semaphore()
    for step in steps:
        pl.semaphore_signal(barrier, inc=1, device_id=place(step), device_id_type=MESH)

    at_row = lax.broadcasted_iota(jnp.int32, (LANES, LANES), 0)
    at_column = lax.broadcasted_iota(jnp.int32, (LANES, LANES), 1)
    reverse = jnp.where(at_row + at_column == LANES - 1, 1.0, 0.0).astype(jnp.bfloat16)

    rhs_sum[...] = jnp.zeros_like(rhs_sum)
    for load in loads[:3]:
        load.wait()

    def dish_step(d, carry):
        weight = gains[d]
        for b in range(blocks_dev):
            series = time_data[d, :, b * LANES:(b + 1) * LANES]
            term = lax.dot_general(
                noise[d], series, (((1,), (1,)), ((), ())),
                preferred_element_type=jnp.float32,
            )
            rhs_sum[b] += weight[b:b + 1, :] * term
        return carry

    def diagonal_step(d, carry):
        upside = jnp.dot(reverse, noise[d], preferred_element_type=jnp.float32)
        skewed = pltpu.roll(upside, 1, 1, stride=1, stride_axis=0)
        turned = jnp.dot(
            skewed.T[0:2 * BAND].astype(jnp.bfloat16), reverse,
            preferred_element_type=jnp.float32,
        )
        diag_wide[d] = turned
        return carry

    group_steps = [step for step in steps if step[1] == 0]
    members = [tm_at[step[0]] * dish + dish_at[step[2]] for step in group_steps]
    row = lax.broadcasted_iota(jnp.int32, (8, LANES), 0)
    tile_rows = jnp.zeros((8, LANES), jnp.int32)
    for b in range(blocks_dev):
        tile = lax.rem(my_tm * (tiles // tm) + coverage[b], tiles)
        tile_rows = jnp.where(row == b, tile, tile_rows)
    tile_send[...] = tile_rows

    lax.fori_loop(0, dishes_dev // 2, dish_step, 0, unroll=4)
    for load in loads[3:]:
        load.wait()
    pl.semaphore_wait(barrier, devices - 1)
    for a in range(1, tm):
        step = (a, 0, 0)
        remote(tile_send, tiles_at.at[my_tm], setup_sems.at[6], setup_sems.at[7], step).start()
        remote(
            points.at[my_tm], points.at[my_tm], setup_sems.at[4], setup_sems.at[5], step
        ).start()
    for step, t in zip(group_steps, members):
        remote(
            precond.at[pl.ds(pl.multiple_of(t * ROWS, ROWS), ROWS), :], pre_got.at[member],
            setup_sems.at[2], setup_sems.at[3], step,
        ).start()
    lax.fori_loop(dishes_dev // 2, dishes_dev, dish_step, 0, unroll=4)
    for b in range(blocks_dev):
        rhs_send[:, b] = rhs_sum[b].T.reshape(group, ROWS, LANES)
    for step, t in zip(group_steps, members):
        remote(
            rhs_send.at[t], rhs_got.at[member], setup_sems.at[0], setup_sems.at[1], step
        ).start()

    lax.fori_loop(0, dishes_dev, diagonal_step, 0, unroll=4)
    for k in range(BAND + 1):
        diag_send[k] = diag_wide[:, k, :].astype(jnp.bfloat16)
    for c in range(1, dish):
        remote(
            diag_send, diags.at[my_dish], setup_sems.at[10], setup_sems.at[11], (0, 0, c)
        ).start()
    lane = lax.broadcasted_iota(jnp.int32, (dishes_dev, LANES), 1)
    slot = [
        jnp.logical_and(
            lane >= my_tm * span_rows + b * ROWS, lane < my_tm * span_rows + (b + 1) * ROWS
        )
        for b in range(blocks_dev)
    ]
    for t in range(group):
        column = jnp.zeros((dishes_dev, LANES), jnp.float32)
        for b in range(blocks_dev):
            turn = lax.rem(my_tm * span_rows + (b * ROWS - t * ROWS + LANES), LANES)
            column = jnp.where(slot[b], pltpu.roll(gains[:, b, :], turn, 1), column)
        gain_send[t] = column
    for step in group_steps:
        t = tm_at[step[0]] * dish + dish_at[step[2]]
        remote(
            gain_send.at[t], gain_got.at[member], setup_sems.at[8], setup_sems.at[9], step
        ).start()
    rhs_got[member] = rhs_send[member]
    pre_got[member] = precond[pl.ds(pl.multiple_of(member * ROWS, ROWS), ROWS), :]
    tiles_at[my_tm] = tile_send[...]
    gain_got[member] = gain_send[member]
    diags[my_dish] = diag_send[...]

    channels = devices * ROWS
    rows_here = pairs * ROWS
    own_rows = prior[my_pair, my_half]
    at_row = lax.broadcasted_iota(jnp.int32, (ROWS, channels), 0)
    at_column = lax.broadcasted_iota(jnp.int32, (ROWS, channels), 1)
    diagonal = jnp.sum(
        jnp.where(at_column == at_row + me * ROWS, own_rows, 0.0), axis=1, keepdims=True
    )

    def tile_row(b):
        one = tiles_at[b // blocks_dev, pl.ds(b % blocks_dev, 1), :]
        return jnp.broadcast_to(one, (ROWS, LANES))

    def back_project(rows):
        parts = [
            jnp.dot(
                rows[b * ROWS:(b + 1) * ROWS], points[b // blocks_dev, b % blocks_dev],
                preferred_element_type=jnp.float32,
            )
            for b in range(blocks)
        ]
        rows_at = [tile_row(b) for b in range(blocks)]
        summed = []
        for t in range(tiles):
            one = jnp.where(rows_at[0] == t, parts[0], 0.0)
            for b in range(1, blocks):
                one = one + jnp.where(rows_at[b] == t, parts[b], 0.0)
            summed.append(one)
        return summed

    wait_bytes(rhs_got.at[pl.ds(0, group - 1)], setup_sems.at[1])
    wait_bytes(pre_got.at[pl.ds(0, group - 1)], setup_sems.at[3])
    if tm > 1:
        wait_bytes(tiles_at.at[pl.ds(0, tm - 1)], setup_sems.at[7])
        wait_bytes(points.at[pl.ds(0, tm - 1)], setup_sems.at[5])
    rhs_list = []
    for k in range(tm):
        span = rhs_got[k * dish]
        for j in range(1, dish):
            span = span + rhs_got[k * dish + j]
        rhs_list.append(span.reshape(span_rows, LANES))
    rhs = jnp.concatenate(rhs_list, axis=0).astype(jnp.bfloat16)
    for t, one in enumerate(back_project(rhs)):
        first = (t % tiles_own) * LANES
        scale = pre_got[t // tiles_own, :, first:first + LANES]
        pre[t] = scale
        state_r[t] = one
        state_u[t] = scale * one
    zero = jnp.zeros((tiles, ROWS, LANES), jnp.float32)
    state_x[...] = zero
    state_p[...] = zero
    tile_p[...] = jnp.zeros_like(tile_p)

    like_steps = [step for step in steps if step[2] % 2 == 0]
    sibling = lax.rem(my_dish + 1, 2)
    sibling_place = {
        "tm": my_tm, "freq": my_freq, "dish": my_dish - my_half + sibling,
    }

    def send_like(src, dst, send, recv):
        for step in like_steps:
            remote(src.at[lax.div(index_of(step), 2)], dst, send, recv, step).start()

    def send_dots(src, dst, send, recv):
        for step in steps:
            remote(src, dst.at[me], send, recv, step).start()
        dst[me] = src[...]

    def sum_of(dots):
        return jnp.sum(jnp.sum(dots[...], axis=0), axis=1, keepdims=True)

    def begin():
        u_send[...] = state_u[...].astype(jnp.bfloat16)
        send_like(u_send, field.at[my_half, my_pair], leg_sems.at[0], leg_sems.at[1])
        field[my_half, my_pair] = u_send[my_pair]
        first = jnp.sum(state_r[...] * state_u[...], axis=0)
        fresh_send[...] = jnp.sum(first, axis=0, keepdims=True)
        send_dots(fresh_send, fresh_got, leg_sems.at[8], leg_sems.at[9])

    def order_prior():
        kept = prior[:, my_half].reshape(rows_here, channels)
        at_row = lax.broadcasted_iota(jnp.int32, (rows_here, channels), 0)
        at_column = lax.broadcasted_iota(jnp.int32, (rows_here, channels), 1)
        channel = (at_row // ROWS) * (2 * ROWS) + my_half * ROWS + at_row % ROWS
        kept = jnp.where(channel == at_column, 0.0, kept).astype(jnp.bfloat16)
        at_row = lax.broadcasted_iota(jnp.int32, (channels, rows_here), 0)
        at_column = lax.broadcasted_iota(jnp.int32, (channels, rows_here), 1)
        wanted = (at_column // ROWS) * (2 * ROWS) + at_column % ROWS
        for part, which in ((same_half, my_half), (other_half, 1 - my_half)):
            pick = jnp.where(at_row == wanted + which * ROWS, 1.0, 0.0).astype(jnp.bfloat16)
            part[...] = jnp.dot(kept, pick, preferred_element_type=jnp.float32).astype(jnp.bfloat16)

    def mix_all():
        for b in range(blocks):
            one = points[b // blocks_dev, b % blocks_dev].astype(jnp.float32)
            turned_points[b] = one.T.astype(jnp.bfloat16)
        wait_bytes(gain_got.at[pl.ds(0, group - 1)], setup_sems.at[9])
        wait_bytes(diags.at[pl.ds(0, dish - 1)], setup_sems.at[11])
        gain_list = []
        for j in range(dish):
            column = gain_got[j]
            for k in range(1, tm):
                column = column + gain_got[k * dish + j]
            gain_list.append(column)
        gain = jnp.concatenate(gain_list, axis=0)
        high, low = halves(gain * gain)
        weights = jnp.concatenate([high, low], axis=0).T.astype(jnp.bfloat16)

        for k in range(BAND + 1):
            one = [diags[j, k] for j in range(dish)]
            stacked = jnp.concatenate(one + one, axis=0)
            one = jnp.dot(weights, stacked, preferred_element_type=jnp.float32)
            mixing[BAND + k] = one
            if k > 0:
                mixing[BAND - k] = pltpu.roll(one, k, 1)

    def iteration(index, energy_old, last=False):
        wait_bytes(field.at[0, pl.ds(0, pairs - 1)], leg_sems.at[1])
        forward = pltpu.make_async_remote_copy(
            src_ref=field.at[my_half], dst_ref=field.at[my_half],
            send_sem=leg_sems.at[2], recv_sem=leg_sems.at[3],
            device_id=sibling_place, device_id_type=MESH,
        )
        forward.start()
        wait_bytes(fresh_got.at[pl.ds(0, devices - 1)], leg_sems.at[9])
        energy = sum_of(fresh_got)
        beta = jnp.where(index == 0, 0.0, energy / energy_old)
        state_p[...] = state_u[...] + beta[None] * state_p[...]
        for b in range(blocks):
            at = tile_row(b)
            seen = jnp.where(at == 0, state_p[0], 0.0)
            for t in range(1, tiles):
                seen = seen + jnp.where(at == t, state_p[t], 0.0)
            model[b * ROWS:(b + 1) * ROWS] = jnp.dot(
                seen.astype(jnp.bfloat16), turned_points[b],
                preferred_element_type=jnp.float32,
            ).astype(jnp.bfloat16).astype(jnp.float32)

        tod = model[...]
        mixed = mixing[BAND] * tod
        for k in range(DIAGS):
            if k != BAND:
                mixed = mixed + mixing[k] * pltpu.roll(tod, (BAND - k) % LANES, 1)

        forward.wait()
        mine = field[my_half].reshape(rows_here, LANES).astype(jnp.float32)
        mine = mine + beta * tile_p[my_half]
        tile_p[my_half] = mine
        theirs = field[1 - my_half].reshape(rows_here, LANES).astype(jnp.float32)
        theirs = theirs + beta * tile_p[1 - my_half]
        tile_p[1 - my_half] = theirs
        applied = jnp.dot(
            same_half[...], mine.astype(jnp.bfloat16), preferred_element_type=jnp.float32
        ) + jnp.dot(
            other_half[...], theirs.astype(jnp.bfloat16), preferred_element_type=jnp.float32
        )
        back_send[...] = applied.reshape(pairs, ROWS, LANES).astype(jnp.bfloat16)
        send_like(back_send, back.at[my_pair], leg_sems.at[4], leg_sems.at[5])
        back[my_pair] = back_send[my_pair]

        curve = jnp.zeros((ROWS, LANES), jnp.float32)
        for t, one in enumerate(back_project(mixed.astype(jnp.bfloat16))):
            here = state_p[t]
            term = one + diagonal * here
            state_w[t] = term
            curve = curve + here * term
        curve_send[...] = jnp.sum(curve, axis=0, keepdims=True) + jnp.sum(
            applied * mine, axis=0, keepdims=True
        )
        send_dots(curve_send, curve_got, leg_sems.at[6], leg_sems.at[7])
        if last:
            for t in range(tiles):
                first = (t % tiles_own) * LANES
                early_send[t // tiles_own, 0, :, first:first + LANES] = state_x[t]
                early_send[t // tiles_own, 1, :, first:first + LANES] = state_p[t]
            for step, t in zip(group_steps, members):
                remote(
                    early_send.at[t], early_got.at[member], setup_sems.at[14],
                    setup_sems.at[15], step,
                ).start()
            early_got[member] = early_send[member]
        wait_bytes(back.at[pl.ds(0, pairs - 1)], leg_sems.at[5])
        wait_bytes(curve_got.at[pl.ds(0, devices - 1)], leg_sems.at[7])
        length = energy / sum_of(curve_got)
        for t in range(tiles):
            operated = state_w[t] + back[t].astype(jnp.float32)
            residual = state_r[t] - length * operated
            if last:
                first = (t % tiles_own) * LANES
                end_send[t // tiles_own, :, first:first + LANES] = residual
            else:
                state_x[t] = state_x[t] + length * state_p[t]
                state_r[t] = residual
                state_u[t] = pre[t] * residual
        if last:
            for step, t in zip(group_steps, members):
                remote(
                    end_send.at[t], end_recv.at[member, 1], setup_sems.at[12],
                    setup_sems.at[13], step,
                ).start()
            end_recv[member, 1] = end_send[member]
        wait_bytes(u_send.at[pl.ds(0, pairs - 1)], leg_sems.at[0])
        wait_bytes(back_send.at[pl.ds(0, pairs - 1)], leg_sems.at[4])
        wait_bytes(curve_got.at[pl.ds(0, devices - 1)], leg_sems.at[6])
        wait_bytes(fresh_got.at[pl.ds(0, devices - 1)], leg_sems.at[8])
        return length if last else energy

    def later(index, energy):
        begin()
        return iteration(index, energy)

    begin()
    order_prior()
    mix_all()
    energy = iteration(0, jnp.ones((1, 1), jnp.float32))
    energy = lax.fori_loop(1, ITERS - 1, later, energy)
    begin()
    length = iteration(ITERS - 1, energy, last=True)

    wait_bytes(early_got.at[pl.ds(0, group - 1)], setup_sems.at[15])
    for t in range(group):
        end_recv[t, 0] = early_got[t, 0] + length * early_got[t, 1]
    wait_bytes(early_send.at[pl.ds(0, group - 1)], setup_sems.at[14])
    wait_bytes(rhs_send.at[pl.ds(0, group - 1)], setup_sems.at[0])
    wait_bytes(pre_got.at[pl.ds(0, group - 1)], setup_sems.at[2])
    for a in range(1, tm):
        wait_bytes(points.at[0], setup_sems.at[4])
        wait_bytes(tile_send, setup_sems.at[6])
    wait_bytes(gain_send.at[pl.ds(0, group - 1)], setup_sems.at[8])
    wait_bytes(diags.at[pl.ds(0, dish - 1)], setup_sems.at[10])
    wait_bytes(end_send.at[pl.ds(0, group - 1)], setup_sems.at[13])
    wait_bytes(end_send.at[pl.ds(0, group - 1)], setup_sems.at[12])


def spread(ends, x_out, r_out, sems):
    copies = [
        pltpu.make_async_copy(
            ends.at[t, i], out.at[pl.ds(t * ROWS, ROWS), :], sems.at[t, i]
        )
        for t in range(ends.shape[0])
        for i, out in enumerate((x_out, r_out))
    ]
    for copy in copies:
        copy.start()
    for copy in copies:
        copy.wait()


def local_body(time_data, pointing, coverage, noise_inv, gains, prior_inv, precond):
    tm, freq, dish = (lax.axis_size(name) for name in ("tm", "freq", "dish"))
    group = tm * dish
    devices = group * freq
    pairs = devices // 2
    dishes_dev, channels_dev, _ = time_data.shape
    channels = prior_inv.shape[0]
    blocks_dev = pointing.shape[0]
    tiles_own = precond.shape[1] // LANES
    tiles = tiles_own * group

    f32, bf16 = jnp.float32, jnp.bfloat16
    state = pltpu.VMEM((tiles, ROWS, LANES), f32)
    half = pltpu.VMEM((pairs * ROWS, pairs * ROWS), bf16)
    leg = pltpu.VMEM((pairs, ROWS, LANES), bf16)
    end = pltpu.VMEM((group, 2, ROWS, tiles_own * LANES), f32)
    rhs = pltpu.VMEM((group, blocks_dev, ROWS, LANES), f32)
    gain = pltpu.VMEM((group, dishes_dev, LANES), f32)
    dots = pltpu.VMEM((1, LANES), f32)
    all_dots = pltpu.VMEM((devices, 1, LANES), f32)
    vmem = pl.BlockSpec(memory_space=pltpu.VMEM)
    hbm = pl.BlockSpec(memory_space=pl.ANY)
    smem = pl.BlockSpec(memory_space=pltpu.SMEM)
    shape = jax.ShapeDtypeStruct(precond.shape, f32)
    ends = pl.pallas_call(
        functools.partial(kernel, (tm, freq, dish)),
        out_shape=jax.ShapeDtypeStruct((group, 2, ROWS, tiles_own * LANES), f32),
        in_specs=[hbm, hbm, smem, hbm, hbm, hbm, hbm],
        out_specs=vmem,
        scratch_shapes=[
            pltpu.VMEM(time_data.shape, bf16),
            pltpu.VMEM(noise_inv.shape, bf16),
            pltpu.VMEM((dishes_dev, blocks_dev, channels_dev), f32),
            pltpu.VMEM((pairs, 2, ROWS, channels), f32),
            pltpu.VMEM(precond.shape, f32),
            pltpu.VMEM((blocks_dev, LANES, channels_dev), f32),
            rhs, rhs, gain, gain,
            pltpu.VMEM((dishes_dev, 2 * BAND, LANES), f32),
            pltpu.VMEM((BAND + 1, dishes_dev, LANES), bf16),
            pltpu.VMEM((dish, BAND + 1, dishes_dev, LANES), bf16),
            pltpu.VMEM((tm,) + pointing.shape, bf16),
            pltpu.VMEM((tm * blocks_dev, LANES, LANES), bf16),
            pltpu.VMEM((8, LANES), jnp.int32),
            pltpu.VMEM((tm, 8, LANES), jnp.int32),
            pltpu.VMEM((group, ROWS, tiles_own * LANES), f32),
            pltpu.VMEM((DIAGS, LANES, LANES), f32),
            pltpu.VMEM((LANES, LANES), f32),
            state, state, state, state, state, state,
            pltpu.VMEM((2, pairs * ROWS, LANES), f32),
            half, half, leg,
            pltpu.VMEM((2, pairs, ROWS, LANES), bf16),
            leg, leg,
            dots, all_dots, dots, all_dots, end, end,
            pltpu.VMEM((group, ROWS, tiles_own * LANES), f32),
            pltpu.SemaphoreType.DMA((6,)),
            pltpu.SemaphoreType.DMA((16,)),
            pltpu.SemaphoreType.DMA((10,)),
        ],
        compiler_params=pltpu.CompilerParams(
            collective_id=0, has_side_effects=True, vmem_limit_bytes=60 * 1024 * 1024
        ),
    )(
        time_data, pointing, coverage, noise_inv, gains.transpose(0, 2, 1),
        prior_inv.reshape(pairs, 2, ROWS, channels), precond,
    )
    return pl.pallas_call(
        spread,
        out_shape=(shape, shape),
        in_specs=[hbm],
        out_specs=(hbm, hbm),
        scratch_shapes=[pltpu.SemaphoreType.DMA((group, 2))],
        compiler_params=pltpu.CompilerParams(vmem_limit_bytes=60 * 1024 * 1024),
    )(ends)


def body(time_data, pointing, coverage, noise_inv, gains, prior_inv, precond):
    group = lax.axis_size("tm") * lax.axis_size("dish")
    devices = group * lax.axis_size("freq")
    fits = (
        prior_inv.shape[0] == devices * ROWS
        and precond.shape[1] * group * 2 == devices * LANES
        and pointing.shape[0] * lax.axis_size("tm") * ROWS == LANES
        and time_data.shape[0] == ROWS
        and ROWS * lax.axis_size("dish") * 2 == LANES
        and time_data.shape[1] == LANES
    )
    run = local_body if fits else general_body
    return run(time_data, pointing, coverage, noise_inv, gains, prior_inv, precond)


def solution(mesh):
    return jax.shard_map(
        body,
        mesh=mesh,
        in_specs=(
            P("dish", "freq", "tm"),
            P("tm", None, None),
            P("tm"),
            P("dish", None, None),
            P("dish", "freq", "tm"),
            P(),
            P("freq", ("tm", "dish")),
        ),
        out_specs=(P("freq", ("tm", "dish")), P("freq", ("tm", "dish"))),
        check_vma=False,
    )
```

```python
import functools

import jax
import jax.numpy as jnp
from jax import lax
from jax.experimental import pallas as pl
from jax.experimental.pallas import tpu as pltpu
from jax.sharding import PartitionSpec as P

ITERS = 4
BAND = 16
DIAGS = 2 * BAND + 1
ROWS = 16
LANES = 128
MESH = pl.DeviceIdType.MESH


def shifted(block, axis, distance):
    devices = range(lax.axis_size(axis))
    route = [((i - distance) % len(devices), i) for i in devices]
    return lax.ppermute(block, axis, route)


def general_body(time_data, pointing, coverage, noise_inv, gains, prior_inv, precond):
    highest = lax.Precision.HIGHEST
    channels_dev = precond.shape[0]
    owned_pixels = precond.shape[1]
    blocks_dev = pointing.shape[0]
    dish_count = lax.axis_size("dish")
    owned_tiles = owned_pixels // 128
    region_tiles = owned_tiles * dish_count
    window_tiles = 2 * region_tiles
    tile_count = jnp.arange(owned_tiles, dtype=jnp.int32)
    first_owned = lax.axis_index("dish") * owned_tiles + tile_count
    wanted = jnp.concatenate([first_owned, first_owned + region_tiles])
    own_hot = (coverage[:, None] == wanted[None, :]).astype(jnp.float32)

    def collect(partial_tod):
        summed = lax.psum(partial_tod, "dish")
        tile_part = jnp.einsum(
            "cbt,bti->cbi",
            summed.astype(jnp.bfloat16),
            pointing,
            preferred_element_type=jnp.float32,
        )
        window = jnp.einsum("cbi,bw->cwi", tile_part, own_hot, precision=highest)
        own_part = window[:, :owned_tiles, :].reshape(channels_dev, owned_pixels)
        ahead_part = window[:, owned_tiles:, :].reshape(channels_dev, owned_pixels)
        arrived = shifted(ahead_part, "tm", 1)
        return own_part + arrived

    def energy_of(residual, scaled):
        return lax.psum(jnp.sum(residual * scaled), ("tm", "freq", "dish"))

    series = time_data.reshape(time_data.shape[0], channels_dev, blocks_dev, 128)
    rhs_weighted = jnp.einsum(
        "dcbs,dst->dcbt", series, noise_inv, preferred_element_type=jnp.float32
    )
    right_side = collect(jnp.sum(gains[:, :, :, None] * rhs_weighted, axis=0))
    estimate = jnp.zeros_like(right_side)
    residual = right_side
    scaled = precond * residual
    direction = scaled
    energy_now = energy_of(residual, scaled)
    for iteration in range(ITERS):
        swapped = lax.all_to_all(direction, "freq", split_axis=1, concat_axis=0, tiled=True)
        applied = jnp.dot(prior_inv, swapped, precision=highest, preferred_element_type=jnp.float32)
        region_map = lax.all_gather(direction.astype(jnp.bfloat16), "dish", axis=1, tiled=True)
        following = shifted(region_map, "tm", -1)
        data_window = jnp.concatenate([region_map, following], axis=1)
        tile_maps = data_window.reshape(channels_dev, window_tiles, 128)[:, coverage, :]
        model_tod = jnp.einsum(
            "cbp,bsp->cbs", tile_maps, pointing, preferred_element_type=jnp.float32
        ).astype(jnp.bfloat16)
        weighted = jnp.einsum(
            "cbs,dst->dcbt", model_tod, noise_inv, preferred_element_type=jnp.float32
        )
        mixed_part = jnp.sum((gains * gains)[:, :, :, None] * weighted, axis=0)
        operated = collect(mixed_part) + lax.all_to_all(
            applied, "freq", split_axis=0, concat_axis=1, tiled=True
        )
        curve_sum = lax.psum(jnp.sum(direction * operated), ("tm", "freq", "dish"))
        step_size = energy_now / curve_sum
        estimate = estimate + step_size * direction
        residual = residual - step_size * operated
        if iteration + 1 < ITERS:
            scaled = precond * residual
            energy_next = energy_of(residual, scaled)
            direction = scaled + energy_next / energy_now * direction
            energy_now = energy_next
    return (estimate, residual)


def halves(value):
    high = value.astype(jnp.bfloat16).astype(jnp.float32)
    return high, value - high


def total(value):
    return jnp.sum(jnp.sum(value, axis=0, keepdims=True), axis=1, keepdims=True)


def kernel(
    sizes, time_hbm, pointing_hbm, coverage, noise_hbm, gains_hbm, prior_hbm,
    precond_hbm, end_recv, time_data, noise, gains, prior, precond, rhs_sum, rhs_send, rhs_got, gain_send, gain_got, diag_wide, diag_send, diags,
    points, turned_points, tile_send, tiles_at, pre_got, mixing, model, state_x, state_r, state_u,
    state_p, state_w, pre, tile_p, same_half, other_half, u_send, field, back_send,
    back, fresh_send, fresh_got, curve_send, curve_got, early_send, early_got, end_send, load_sems, setup_sems, leg_sems,
):
    tm, freq, dish = sizes
    group = tm * dish
    devices = group * freq
    dishes_dev, channels_dev, _ = time_data.shape
    blocks_dev = pointing_hbm.shape[0]
    blocks = tm * blocks_dev
    span_rows = blocks_dev * ROWS
    tiles_own = precond.shape[1] // LANES
    tiles = tiles_own * group
    pairs = devices // 2
    my_tm = lax.axis_index("tm")
    my_freq = lax.axis_index("freq")
    my_dish = lax.axis_index("dish")
    member = my_tm * dish + my_dish
    me = my_freq * group + member
    my_pair = lax.div(me, 2)
    my_half = lax.rem(me, 2)

    tm_at = [lax.rem(my_tm + step, tm) for step in range(tm)]
    freq_at = [lax.rem(my_freq + step, freq) for step in range(freq)]
    dish_at = [lax.rem(my_dish + step, dish) for step in range(dish)]
    steps = [
        (a, b, c) for b in range(freq) for a in range(tm) for c in range(dish)
    ]
    steps = sorted(steps[1:], key=lambda s: (-min(s[1], freq - s[1]), s))

    def index_of(step):
        a, b, c = step
        return freq_at[b] * group + tm_at[a] * dish + dish_at[c]

    def place(step):
        a, b, c = step
        return {"tm": tm_at[a], "freq": freq_at[b], "dish": dish_at[c]}

    def remote(src, dst, send, recv, step):
        return pltpu.make_async_remote_copy(
            src_ref=src, dst_ref=dst, send_sem=send, recv_sem=recv,
            device_id=place(step), device_id_type=MESH,
        )

    def wait_bytes(ref, sem):
        pltpu.make_async_copy(ref, ref, sem).wait()

    loads = [
        pltpu.make_async_copy(src, dst, load_sems.at[i])
        for i, (src, dst) in enumerate(
            [
                (noise_hbm, noise), (gains_hbm, gains), (time_hbm, time_data),
                (pointing_hbm, points.at[my_tm]), (precond_hbm, precond), (prior_hbm, prior),
            ]
        )
    ]
    for load in loads:
        load.start()
    barrier = pltpu.get_barrier_semaphore()
    for step in steps:
        pl.semaphore_signal(barrier, inc=1, device_id=place(step), device_id_type=MESH)

    at_row = lax.broadcasted_iota(jnp.int32, (LANES, LANES), 0)
    at_column = lax.broadcasted_iota(jnp.int32, (LANES, LANES), 1)
    reverse = jnp.where(at_row + at_column == LANES - 1, 1.0, 0.0).astype(jnp.bfloat16)

    rhs_sum[...] = jnp.zeros_like(rhs_sum)
    for load in loads[:3]:
        load.wait()

    def dish_step(d, carry):
        weight = gains[d]
        for b in range(blocks_dev):
            series = time_data[d, :, b * LANES:(b + 1) * LANES]
            term = lax.dot_general(
                noise[d], series, (((1,), (1,)), ((), ())),
                preferred_element_type=jnp.float32,
            )
            rhs_sum[b] += weight[b:b + 1, :] * term
        return carry

    def diagonal_step(d, carry):
        upside = jnp.dot(reverse, noise[d], preferred_element_type=jnp.float32)
        skewed = pltpu.roll(upside, 1, 1, stride=1, stride_axis=0)
        turned = jnp.dot(
            skewed.T[0:2 * BAND].astype(jnp.bfloat16), reverse,
            preferred_element_type=jnp.float32,
        )
        diag_wide[d] = turned
        return carry

    group_steps = [step for step in steps if step[1] == 0]
    members = [tm_at[step[0]] * dish + dish_at[step[2]] for step in group_steps]
    row = lax.broadcasted_iota(jnp.int32, (8, LANES), 0)
    tile_rows = jnp.zeros((8, LANES), jnp.int32)
    for b in range(blocks_dev):
        tile = lax.rem(my_tm * (tiles // tm) + coverage[b], tiles)
        tile_rows = jnp.where(row == b, tile, tile_rows)
    tile_send[...] = tile_rows

    lax.fori_loop(0, dishes_dev // 2, dish_step, 0, unroll=4)
    for load in loads[3:]:
        load.wait()
    pl.semaphore_wait(barrier, devices - 1)
    for a in range(1, tm):
        step = (a, 0, 0)
        remote(tile_send, tiles_at.at[my_tm], setup_sems.at[6], setup_sems.at[7], step).start()
        remote(
            points.at[my_tm], points.at[my_tm], setup_sems.at[4], setup_sems.at[5], step
        ).start()
    for step, t in zip(group_steps, members):
        remote(
            precond.at[pl.ds(pl.multiple_of(t * ROWS, ROWS), ROWS), :], pre_got.at[member],
            setup_sems.at[2], setup_sems.at[3], step,
        ).start()
    lax.fori_loop(dishes_dev // 2, dishes_dev, dish_step, 0, unroll=4)
    for b in range(blocks_dev):
        rhs_send[:, b] = rhs_sum[b].T.reshape(group, ROWS, LANES)
    for step, t in zip(group_steps, members):
        remote(
            rhs_send.at[t], rhs_got.at[member], setup_sems.at[0], setup_sems.at[1], step
        ).start()

    lax.fori_loop(0, dishes_dev, diagonal_step, 0, unroll=4)
    for k in range(BAND + 1):
        diag_send[k] = diag_wide[:, k, :].astype(jnp.bfloat16)
    for c in range(1, dish):
        remote(
            diag_send, diags.at[my_dish], setup_sems.at[10], setup_sems.at[11], (0, 0, c)
        ).start()
    lane = lax.broadcasted_iota(jnp.int32, (dishes_dev, LANES), 1)
    slot = [
        jnp.logical_and(
            lane >= my_tm * span_rows + b * ROWS, lane < my_tm * span_rows + (b + 1) * ROWS
        )
        for b in range(blocks_dev)
    ]
    for t in range(group):
        column = jnp.zeros((dishes_dev, LANES), jnp.float32)
        for b in range(blocks_dev):
            turn = lax.rem(my_tm * span_rows + (b * ROWS - t * ROWS + LANES), LANES)
            column = jnp.where(slot[b], pltpu.roll(gains[:, b, :], turn, 1), column)
        gain_send[t] = column
    for step in group_steps:
        t = tm_at[step[0]] * dish + dish_at[step[2]]
        remote(
            gain_send.at[t], gain_got.at[member], setup_sems.at[8], setup_sems.at[9], step
        ).start()
    rhs_got[member] = rhs_send[member]
    pre_got[member] = precond[pl.ds(pl.multiple_of(member * ROWS, ROWS), ROWS), :]
    tiles_at[my_tm] = tile_send[...]
    gain_got[member] = gain_send[member]
    diags[my_dish] = diag_send[...]

    channels = devices * ROWS
    rows_here = pairs * ROWS
    own_rows = prior[my_pair, my_half]
    at_row = lax.broadcasted_iota(jnp.int32, (ROWS, channels), 0)
    at_column = lax.broadcasted_iota(jnp.int32, (ROWS, channels), 1)
    diagonal = jnp.sum(
        jnp.where(at_column == at_row + me * ROWS, own_rows, 0.0), axis=1, keepdims=True
    )

    def tile_row(b):
        one = tiles_at[b // blocks_dev, pl.ds(b % blocks_dev, 1), :]
        return jnp.broadcast_to(one, (ROWS, LANES))

    def back_project(rows):
        parts = [
            jnp.dot(
                rows[b * ROWS:(b + 1) * ROWS], points[b // blocks_dev, b % blocks_dev],
                preferred_element_type=jnp.float32,
            )
            for b in range(blocks)
        ]
        rows_at = [tile_row(b) for b in range(blocks)]
        summed = []
        for t in range(tiles):
            one = jnp.where(rows_at[0] == t, parts[0], 0.0)
            for b in range(1, blocks):
                one = one + jnp.where(rows_at[b] == t, parts[b], 0.0)
            summed.append(one)
        return summed

    wait_bytes(rhs_got.at[pl.ds(0, group - 1)], setup_sems.at[1])
    wait_bytes(pre_got.at[pl.ds(0, group - 1)], setup_sems.at[3])
    if tm > 1:
        wait_bytes(tiles_at.at[pl.ds(0, tm - 1)], setup_sems.at[7])
        wait_bytes(points.at[pl.ds(0, tm - 1)], setup_sems.at[5])
    rhs_list = []
    for k in range(tm):
        span = rhs_got[k * dish]
        for j in range(1, dish):
            span = span + rhs_got[k * dish + j]
        rhs_list.append(span.reshape(span_rows, LANES))
    rhs = jnp.concatenate(rhs_list, axis=0).astype(jnp.bfloat16)
    for t, one in enumerate(back_project(rhs)):
        first = (t % tiles_own) * LANES
        scale = pre_got[t // tiles_own, :, first:first + LANES]
        pre[t] = scale
        state_r[t] = one
        state_u[t] = scale * one
    zero = jnp.zeros((tiles, ROWS, LANES), jnp.float32)
    state_x[...] = zero
    state_p[...] = zero
    tile_p[...] = jnp.zeros_like(tile_p)

    like_steps = [step for step in steps if step[2] % 2 == 0]
    sibling = lax.rem(my_dish + 1, 2)
    sibling_place = {
        "tm": my_tm, "freq": my_freq, "dish": my_dish - my_half + sibling,
    }

    def send_like(src, dst, send, recv):
        for step in like_steps:
            remote(src.at[lax.div(index_of(step), 2)], dst, send, recv, step).start()

    def send_dots(src, dst, send, recv):
        for step in steps:
            remote(src, dst.at[me], send, recv, step).start()
        dst[me] = src[...]

    def sum_of(dots):
        return jnp.sum(jnp.sum(dots[...], axis=0), axis=1, keepdims=True)

    def begin():
        u_send[...] = state_u[...].astype(jnp.bfloat16)
        send_like(u_send, field.at[my_half, my_pair], leg_sems.at[0], leg_sems.at[1])
        field[my_half, my_pair] = u_send[my_pair]
        first = jnp.sum(state_r[...] * state_u[...], axis=0)
        fresh_send[...] = jnp.sum(first, axis=0, keepdims=True)
        send_dots(fresh_send, fresh_got, leg_sems.at[8], leg_sems.at[9])

    def order_prior():
        kept = prior[:, my_half].reshape(rows_here, channels)
        at_row = lax.broadcasted_iota(jnp.int32, (rows_here, channels), 0)
        at_column = lax.broadcasted_iota(jnp.int32, (rows_here, channels), 1)
        channel = (at_row // ROWS) * (2 * ROWS) + my_half * ROWS + at_row % ROWS
        kept = jnp.where(channel == at_column, 0.0, kept).astype(jnp.bfloat16)
        at_row = lax.broadcasted_iota(jnp.int32, (channels, rows_here), 0)
        at_column = lax.broadcasted_iota(jnp.int32, (channels, rows_here), 1)
        wanted = (at_column // ROWS) * (2 * ROWS) + at_column % ROWS
        for part, which in ((same_half, my_half), (other_half, 1 - my_half)):
            pick = jnp.where(at_row == wanted + which * ROWS, 1.0, 0.0).astype(jnp.bfloat16)
            part[...] = jnp.dot(kept, pick, preferred_element_type=jnp.float32).astype(jnp.bfloat16)

    def mix_all():
        for b in range(blocks):
            one = points[b // blocks_dev, b % blocks_dev].astype(jnp.float32)
            turned_points[b] = one.T.astype(jnp.bfloat16)
        wait_bytes(gain_got.at[pl.ds(0, group - 1)], setup_sems.at[9])
        wait_bytes(diags.at[pl.ds(0, dish - 1)], setup_sems.at[11])
        gain_list = []
        for j in range(dish):
            column = gain_got[j]
            for k in range(1, tm):
                column = column + gain_got[k * dish + j]
            gain_list.append(column)
        gain = jnp.concatenate(gain_list, axis=0)
        high, low = halves(gain * gain)
        weights = jnp.concatenate([high, low], axis=0).T.astype(jnp.bfloat16)

        for k in range(BAND + 1):
            one = [diags[j, k] for j in range(dish)]
            stacked = jnp.concatenate(one + one, axis=0)
            one = jnp.dot(weights, stacked, preferred_element_type=jnp.float32)
            mixing[BAND + k] = one
            if k > 0:
                mixing[BAND - k] = pltpu.roll(one, k, 1)

    def iteration(index, energy_old, last=False):
        wait_bytes(field.at[0, pl.ds(0, pairs - 1)], leg_sems.at[1])
        forward = pltpu.make_async_remote_copy(
            src_ref=field.at[my_half], dst_ref=field.at[my_half],
            send_sem=leg_sems.at[2], recv_sem=leg_sems.at[3],
            device_id=sibling_place, device_id_type=MESH,
        )
        forward.start()
        wait_bytes(fresh_got.at[pl.ds(0, devices - 1)], leg_sems.at[9])
        energy = sum_of(fresh_got)
        beta = jnp.where(index == 0, 0.0, energy / energy_old)
        state_p[...] = state_u[...] + beta[None] * state_p[...]
        for b in range(blocks):
            at = tile_row(b)
            seen = jnp.where(at == 0, state_p[0], 0.0)
            for t in range(1, tiles):
                seen = seen + jnp.where(at == t, state_p[t], 0.0)
            model[b * ROWS:(b + 1) * ROWS] = jnp.dot(
                seen.astype(jnp.bfloat16), turned_points[b],
                preferred_element_type=jnp.float32,
            ).astype(jnp.bfloat16).astype(jnp.float32)

        tod = model[...]
        mixed = mixing[BAND] * tod
        for k in range(DIAGS):
            if k != BAND:
                mixed = mixed + mixing[k] * pltpu.roll(tod, (BAND - k) % LANES, 1)

        forward.wait()
        mine = field[my_half].reshape(rows_here, LANES).astype(jnp.float32)
        mine = mine + beta * tile_p[my_half]
        tile_p[my_half] = mine
        theirs = field[1 - my_half].reshape(rows_here, LANES).astype(jnp.float32)
        theirs = theirs + beta * tile_p[1 - my_half]
        tile_p[1 - my_half] = theirs
        applied = jnp.dot(
            same_half[...], mine.astype(jnp.bfloat16), preferred_element_type=jnp.float32
        ) + jnp.dot(
            other_half[...], theirs.astype(jnp.bfloat16), preferred_element_type=jnp.float32
        )
        back_send[...] = applied.reshape(pairs, ROWS, LANES).astype(jnp.bfloat16)
        send_like(back_send, back.at[my_pair], leg_sems.at[4], leg_sems.at[5])
        back[my_pair] = back_send[my_pair]

        curve = jnp.zeros((ROWS, LANES), jnp.float32)
        for t, one in enumerate(back_project(mixed.astype(jnp.bfloat16))):
            here = state_p[t]
            term = one + diagonal * here
            state_w[t] = term
            curve = curve + here * term
        curve_send[...] = jnp.sum(curve, axis=0, keepdims=True) + jnp.sum(
            applied * mine, axis=0, keepdims=True
        )
        send_dots(curve_send, curve_got, leg_sems.at[6], leg_sems.at[7])
        if last:
            for t in range(tiles):
                first = (t % tiles_own) * LANES
                early_send[t // tiles_own, 0, :, first:first + LANES] = state_x[t]
                early_send[t // tiles_own, 1, :, first:first + LANES] = state_p[t]
            for step, t in zip(group_steps, members):
                remote(
                    early_send.at[t], early_got.at[member], setup_sems.at[14],
                    setup_sems.at[15], step,
                ).start()
            early_got[member] = early_send[member]
        wait_bytes(back.at[pl.ds(0, pairs - 1)], leg_sems.at[5])
        wait_bytes(curve_got.at[pl.ds(0, devices - 1)], leg_sems.at[7])
        length = energy / sum_of(curve_got)
        for t in range(tiles):
            operated = state_w[t] + back[t].astype(jnp.float32)
            residual = state_r[t] - length * operated
            if last:
                first = (t % tiles_own) * LANES
                end_send[t // tiles_own, :, first:first + LANES] = residual
            else:
                state_x[t] = state_x[t] + length * state_p[t]
                state_r[t] = residual
                state_u[t] = pre[t] * residual
        if last:
            for step, t in zip(group_steps, members):
                remote(
                    end_send.at[t], end_recv.at[member, 1], setup_sems.at[12],
                    setup_sems.at[13], step,
                ).start()
            end_recv[member, 1] = end_send[member]
        wait_bytes(u_send.at[pl.ds(0, pairs - 1)], leg_sems.at[0])
        wait_bytes(back_send.at[pl.ds(0, pairs - 1)], leg_sems.at[4])
        wait_bytes(curve_got.at[pl.ds(0, devices - 1)], leg_sems.at[6])
        wait_bytes(fresh_got.at[pl.ds(0, devices - 1)], leg_sems.at[8])
        return length if last else energy

    def later(index, energy):
        begin()
        return iteration(index, energy)

    begin()
    order_prior()
    mix_all()
    energy = iteration(0, jnp.ones((1, 1), jnp.float32))
    energy = lax.fori_loop(1, ITERS - 1, later, energy)
    begin()
    length = iteration(ITERS - 1, energy, last=True)

    wait_bytes(early_got.at[pl.ds(0, group - 1)], setup_sems.at[15])
    for t in range(group):
        end_recv[t, 0] = early_got[t, 0] + length * early_got[t, 1]
    wait_bytes(early_send.at[pl.ds(0, group - 1)], setup_sems.at[14])
    wait_bytes(rhs_send.at[pl.ds(0, group - 1)], setup_sems.at[0])
    wait_bytes(pre_got.at[pl.ds(0, group - 1)], setup_sems.at[2])
    for a in range(1, tm):
        wait_bytes(points.at[0], setup_sems.at[4])
        wait_bytes(tile_send, setup_sems.at[6])
    wait_bytes(gain_send.at[pl.ds(0, group - 1)], setup_sems.at[8])
    wait_bytes(diags.at[pl.ds(0, dish - 1)], setup_sems.at[10])
    wait_bytes(end_send.at[pl.ds(0, group - 1)], setup_sems.at[13])
    wait_bytes(end_send.at[pl.ds(0, group - 1)], setup_sems.at[12])


def spread(ends, x_out, r_out):
    for t in range(ends.shape[0]):
        x_out[t * ROWS:(t + 1) * ROWS] = ends[t, 0]
        r_out[t * ROWS:(t + 1) * ROWS] = ends[t, 1]


def local_body(time_data, pointing, coverage, noise_inv, gains, prior_inv, precond):
    tm, freq, dish = (lax.axis_size(name) for name in ("tm", "freq", "dish"))
    group = tm * dish
    devices = group * freq
    pairs = devices // 2
    dishes_dev, channels_dev, _ = time_data.shape
    channels = prior_inv.shape[0]
    blocks_dev = pointing.shape[0]
    tiles_own = precond.shape[1] // LANES
    tiles = tiles_own * group

    f32, bf16 = jnp.float32, jnp.bfloat16
    state = pltpu.VMEM((tiles, ROWS, LANES), f32)
    half = pltpu.VMEM((pairs * ROWS, pairs * ROWS), bf16)
    leg = pltpu.VMEM((pairs, ROWS, LANES), bf16)
    end = pltpu.VMEM((group, 2, ROWS, tiles_own * LANES), f32)
    rhs = pltpu.VMEM((group, blocks_dev, ROWS, LANES), f32)
    gain = pltpu.VMEM((group, dishes_dev, LANES), f32)
    dots = pltpu.VMEM((1, LANES), f32)
    all_dots = pltpu.VMEM((devices, 1, LANES), f32)
    vmem = pl.BlockSpec(memory_space=pltpu.VMEM)
    hbm = pl.BlockSpec(memory_space=pl.ANY)
    smem = pl.BlockSpec(memory_space=pltpu.SMEM)
    shape = jax.ShapeDtypeStruct(precond.shape, f32)
    ends = pl.pallas_call(
        functools.partial(kernel, (tm, freq, dish)),
        out_shape=jax.ShapeDtypeStruct((group, 2, ROWS, tiles_own * LANES), f32),
        in_specs=[hbm, hbm, smem, hbm, hbm, hbm, hbm],
        out_specs=vmem,
        scratch_shapes=[
            pltpu.VMEM(time_data.shape, bf16),
            pltpu.VMEM(noise_inv.shape, bf16),
            pltpu.VMEM((dishes_dev, blocks_dev, channels_dev), f32),
            pltpu.VMEM((pairs, 2, ROWS, channels), f32),
            pltpu.VMEM(precond.shape, f32),
            pltpu.VMEM((blocks_dev, LANES, channels_dev), f32),
            rhs, rhs, gain, gain,
            pltpu.VMEM((dishes_dev, 2 * BAND, LANES), f32),
            pltpu.VMEM((BAND + 1, dishes_dev, LANES), bf16),
            pltpu.VMEM((dish, BAND + 1, dishes_dev, LANES), bf16),
            pltpu.VMEM((tm,) + pointing.shape, bf16),
            pltpu.VMEM((tm * blocks_dev, LANES, LANES), bf16),
            pltpu.VMEM((8, LANES), jnp.int32),
            pltpu.VMEM((tm, 8, LANES), jnp.int32),
            pltpu.VMEM((group, ROWS, tiles_own * LANES), f32),
            pltpu.VMEM((DIAGS, LANES, LANES), f32),
            pltpu.VMEM((LANES, LANES), f32),
            state, state, state, state, state, state,
            pltpu.VMEM((2, pairs * ROWS, LANES), f32),
            half, half, leg,
            pltpu.VMEM((2, pairs, ROWS, LANES), bf16),
            leg, leg,
            dots, all_dots, dots, all_dots, end, end,
            pltpu.VMEM((group, ROWS, tiles_own * LANES), f32),
            pltpu.SemaphoreType.DMA((6,)),
            pltpu.SemaphoreType.DMA((16,)),
            pltpu.SemaphoreType.DMA((10,)),
        ],
        compiler_params=pltpu.CompilerParams(
            collective_id=0, has_side_effects=True, vmem_limit_bytes=60 * 1024 * 1024
        ),
    )(
        time_data, pointing, coverage, noise_inv, gains.transpose(0, 2, 1),
        prior_inv.reshape(pairs, 2, ROWS, channels), precond,
    )
    return pl.pallas_call(
        spread, out_shape=(shape, shape), in_specs=[vmem], out_specs=(vmem, vmem)
    )(ends)


def body(time_data, pointing, coverage, noise_inv, gains, prior_inv, precond):
    group = lax.axis_size("tm") * lax.axis_size("dish")
    devices = group * lax.axis_size("freq")
    fits = (
        prior_inv.shape[0] == devices * ROWS
        and precond.shape[1] * group * 2 == devices * LANES
        and pointing.shape[0] * lax.axis_size("tm") * ROWS == LANES
        and time_data.shape[0] == ROWS
        and ROWS * lax.axis_size("dish") * 2 == LANES
        and time_data.shape[1] == LANES
    )
    run = local_body if fits else general_body
    return run(time_data, pointing, coverage, noise_inv, gains, prior_inv, precond)


def solution(mesh):
    return jax.shard_map(
        body,
        mesh=mesh,
        in_specs=(
            P("dish", "freq", "tm"),
            P("tm", None, None),
            P("tm"),
            P("dish", None, None),
            P("dish", "freq", "tm"),
            P(),
            P("freq", ("tm", "dish")),
        ),
        out_specs=(P("freq", ("tm", "dish")), P("freq", ("tm", "dish"))),
        check_vma=False,
    )
```
